512 devices in a mesh: tx: 32 (over x, z_lo, core), slab: 16 (over z_hi, y).
Axes of the slice: x: 4, y: 4, z: 16 (z_hi: 4, z_lo: 4; z = z_hi * 4 + z_lo), core: 2. Of those that a mesh axis runs over, the one named last changes fastest.
Arguments:
- fwd_field: float32 [32, 6, 256, 32, 128], P('tx', None, 'slab'), may hold values from -6 to 6
- adj_prev: float32 [32, 6, 256, 32, 128], P('tx', None, 'slab'), may hold values from -4 to 4
- sigma: float32 [256, 32, 128], P('slab'), may hold values from 0.1 to 10
- omega: float32 [32], P('tx'), may hold values from 0.3 to 3
- res_vals: float32 [32, 6, 4096], P('tx', None, 'slab'), may hold values from -6 to 6
- rec_slab: int32 [32, 4096, 1], P('tx', 'slab'), may hold values from 0 to 15; in each aligned block of 256 rows (0 to 255, 256 to 511, ..., all dimensions but the last counted through in order) at most 32 rows name the same one
- rec_cell: int32 [32, 4096], P('tx', 'slab'), may hold values from 0 to 65535
Outputs:
- adjoint: float32 [32, 6, 256, 32, 128], P('tx', None, 'slab')
- gradient: float32 [256, 32, 128], P('slab', 'tx')
The draws below stay inside these ranges and needn't reach their ends.
Inputs may be any that keep to these rules, and one draw needn't show every extreme that they name: `rec_slab`: among one transmitter's receivers held by one index of slab (aligned blocks of 256), at most 32 name the same slab, and some block reaches 32.
All inputs are finite; a program needn't handle non-finite values.
Results may differ from the reference program's by a relative error of at most 0.0001.
Values sent between devices are 32-bit elements; how exact they have to be, the bound alone decides.
No kernel may reach another device: no remote copies, remote signals or barrier semaphores. Data moves between devices by JAX's collectives and lax.ppermute only.
A program may use at most 128 MiB of HBM per device.

```python
import math
import jax
import jax.numpy as jnp
import numpy as np
from jax import lax

SX = 16
NY = 32
NZ = 128
REC_DEV = 256
SWEEPS = 3
CAP = 32
TXG = 32
NX = 256
RECS = 4096
N_SLAB = 16


def place_ends(result, key, least, largest):
    place = [jax.random.randint(jax.random.fold_in(key, axis), (), 0, length) for axis, length in enumerate(result.shape)]
    longest = result.shape.index(max(result.shape))
    next_to = place[:longest] + [(place[longest] + 1) % result.shape[longest]] + place[longest + 1:]
    return result.at[tuple(place)].set(least).at[tuple(next_to)].set(largest)


def block_levels(key, shape, pieces, smallest, largest):
    gain = 1.0
    for dim, shards_of in pieces:
        steps = jax.random.uniform(jax.random.fold_in(jax.random.fold_in(key, 6), dim), (shards_of,), jnp.float32, smallest / len(pieces), largest / len(pieces))
        gain = gain * jnp.repeat(jnp.exp(steps), shape[dim] // shards_of).reshape((-1,) + (1,) * (len(shape) - 1 - dim))
    return gain


def deal_out(stream_key, own, number, rows, number_of, top, reach, lean):
    order = jax.random.permutation(stream_key, number_of)
    crowded, common = shares(number_of, rows * top, reach, lean, True), shares(number_of, rows * top, reach, lean, False)
    places = jnp.arange(number_of)

    def named(sizes, offset_by):
        used = int((sizes > 0).sum())
        fixed = max(1, used // 4)
        shifted = fixed + (places - fixed + offset_by * (used - fixed)) % max(1, number_of - fixed)
        return jnp.zeros((number_of,), jnp.int32).at[order[jnp.where(places < fixed, places, shifted)]].set(jnp.asarray(sizes, jnp.int32))

    sizes = jnp.where(number % 4 == 0, named(crowded, number // 4), named(common, number - number // 4 - 1))
    mixed = jax.random.permutation(jax.random.fold_in(own, 3), number_of)
    giver, taker = mixed[0:number_of // 2 * 2:2], mixed[1:number_of // 2 * 2:2]
    margin = jnp.minimum(sizes[giver] - 1, reach - sizes[taker]) // 2
    margin = jnp.where((giver == order[0]) | (taker == order[0]) | (sizes[taker] == 0), 0, jnp.maximum(margin, 0))
    shifted = jax.random.randint(jax.random.fold_in(own, 4), (number_of // 2,), 0, 1 << 20) % (margin + 1)
    sizes = sizes.at[giver].add(-shifted).at[taker].add(shifted)
    members = jnp.searchsorted(jnp.cumsum(sizes), jnp.arange(rows * top), side="right").astype(jnp.int32)
    grid = members.reshape(top, rows).T
    grid = grid[jax.random.permutation(jax.random.fold_in(own, 1), rows)]
    offset_by = jax.random.randint(jax.random.fold_in(own, 2), (rows, 1), 0, top)
    return jnp.take_along_axis(grid, (jnp.arange(top)[None, :] + offset_by) % top, axis=1)


def shares(amount, total, limit, slope, full):
    weights = [(1 << 20) // math.isqrt(grade ** slope) + 1 for grade in range(1, amount + 1)]
    largest = limit if full else min(limit, max(-(-total // amount), total * weights[0] // sum(weights)))
    least = 1 if total - largest >= amount - 1 else 0
    counts, surplus = [largest] + [least] * (amount - 1), total - largest - least * (amount - 1)
    while surplus > 0:
        movable = [i for i in range(1, amount) if counts[i] < largest] or [i for i in range(1, amount) if counts[i] < limit]
        mass, left = sum([weights[i] for i in movable]), surplus
        for i in movable:
            extra = min(limit - counts[i], max(1, left * weights[i] // mass), surplus)
            counts[i] = counts[i] + extra
            surplus = surplus - extra
    return np.array(counts)


def gaussian(own_key, dims, deviation, reach, shards=(), dtype=jnp.bfloat16):
    array = deviation * jax.random.normal(own_key, dims, jnp.float32)
    if shards:
        array = array * block_levels(own_key, dims, shards, -0.22, 0.18)
    return jnp.clip(array, -reach, reach).astype(dtype)


def setup_inputs(seed: int = 0) -> dict:
    seeds = jax.random.split(jax.random.key(seed), 8)
    fwd_field = gaussian(seeds[0], (TXG, 6, NX, NY, NZ), 1.0, 6.0, ((0, 32), (2, 16)), jnp.float32)
    adj_prev = gaussian(seeds[1], (TXG, 6, NX, NY, NZ), 0.5, 4.0, ((0, 32), (2, 16)), jnp.float32)
    sigma = jnp.clip(jnp.exp(math.log(10.0) - 4.6051702 * jax.random.uniform(seeds[2], (NX, NY, NZ), jnp.float32) ** block_levels(seeds[2], (NX, NY, NZ), ((0, 16),), -0.2, 0.2)), 0.1, 10.0)
    omega = jnp.clip(jnp.exp(math.log(3.0) - 2.3025851 * jax.random.uniform(seeds[3], (TXG,), jnp.float32) ** block_levels(seeds[3], (TXG,), ((0, 32),), -0.2, 0.2)), 0.3, 3.0)
    res_vals = gaussian(seeds[4], (TXG, 6, RECS), 1.0, 6.0, ((0, 32), (2, 16)), jnp.float32)
    rec_slab_keys = jax.random.split(jax.random.fold_in(seeds[5], 1), TXG * RECS // REC_DEV)
    rec_slab_turns = jax.random.permutation(jax.random.fold_in(seeds[5], 3), TXG * RECS // REC_DEV)
    rec_slab = jax.vmap(lambda own, number: deal_out(jax.random.fold_in(seeds[5], 2), own, number, REC_DEV, N_SLAB, 1, CAP, 2))(rec_slab_keys, rec_slab_turns).reshape((TXG, RECS, 1))
    rec_cell = place_ends(jax.random.randint(seeds[6], (TXG, RECS), 0, SX * NY * NZ), jax.random.fold_in(seeds[6], 1), 0, (SX * NY * NZ) - 1).astype(jnp.int32)
    return {"fwd_field": fwd_field, "adj_prev": adj_prev, "sigma": sigma, "omega": omega, "res_vals": res_vals, "rec_slab": rec_slab, "rec_cell": rec_cell}


def relax_ref(field, source, coef_a, coef_b):
    padded = jnp.pad(field, ((0, 0), (1, 1), (1, 1), (1, 1)))
    beside = padded[:, 2:, 1:-1, 1:-1] + padded[:, :-2, 1:-1, 1:-1]
    beside = beside + padded[:, 1:-1, 2:, 1:-1] + padded[:, 1:-1, :-2, 1:-1]
    beside = beside + padded[:, 1:-1, 1:-1, 2:] + padded[:, 1:-1, 1:-1, :-2]
    rhs = source + beside
    real_part = rhs[:3]
    imag_part = rhs[3:]
    return jnp.concatenate([coef_a * real_part - coef_b * imag_part, coef_a * imag_part + coef_b * real_part], 0)

def reference(fwd_field, adj_prev, sigma, omega, res_vals, rec_slab, rec_cell):
    cells = SX * NY * NZ

    def one_pair(total, items):
        fwd_one, prev_one, om, vals, slabs, offs = items
        flat = slabs[:, 0] * cells + offs
        source = jnp.zeros((6, NX * NY * NZ), jnp.float32).at[:, flat].add(vals)
        source = source.reshape(6, NX, NY, NZ)
        beta = om * sigma
        den = 36.0 + beta * beta
        coef_a = 6.0 / den
        coef_b = beta / den
        field = prev_one
        for sweep in range(SWEEPS):
            field = relax_ref(field, source, coef_a, coef_b)
        term = om * lax.optimization_barrier(jnp.sum(fwd_one[:3] * field[3:] + fwd_one[3:] * field[:3], axis=0))
        return (total + term, field)
    start = jnp.zeros((NX, NY, NZ), jnp.float32)
    total, adjoint = lax.scan(one_pair, start, (fwd_field, adj_prev, omega, res_vals, rec_slab, rec_cell))
    gradient = total * (1.0 / jnp.sqrt(jnp.float32(3 * TXG)))
    return (adjoint, gradient)
```

```python
import functools

import jax
import jax.numpy as jnp
from jax import lax
from jax.experimental import pallas as pl
from jax.experimental.pallas import tpu as pltpu
from jax.sharding import PartitionSpec as P

SWEEPS = 3
CAP = 32
LANES = 128
NT = (((1,), (1,)), ((), ()))


def dot_nt(a, b):
    return lax.dot_general(a, b, NT, preferred_element_type=jnp.float32)


def split_3(value):
    high = value.astype(jnp.bfloat16)
    rest = value - high.astype(jnp.float32)
    middle = rest.astype(jnp.bfloat16)
    low = (rest - middle.astype(jnp.float32)).astype(jnp.bfloat16)
    return high, middle, low


def ones_where(mask):
    return jnp.where(mask, 1.0, 0.0).astype(jnp.bfloat16)


def pack_kernel(slabs, vals_ref, slab_ref, cell_ref, out_ref, rows_ref):
    count = vals_ref.shape[1]
    rows_ref[...] = jnp.zeros_like(rows_ref)
    rows_ref[0:6, :] = vals_ref[...]
    rows_ref[6:7, :] = cell_ref[...].astype(jnp.float32)
    target = slab_ref[...]
    member = ones_where(lax.broadcasted_iota(jnp.int32, (slabs, count), 0) == target)
    before = ones_where(
        lax.broadcasted_iota(jnp.int32, (count, count), 0)
        < lax.broadcasted_iota(jnp.int32, (count, count), 1)
    )
    ahead = jnp.dot(member, before, preferred_element_type=jnp.float32)
    rank = jnp.sum(ahead * member.astype(jnp.float32), axis=0, keepdims=True)
    key = (target + 1) * CAP + rank.astype(jnp.int32)
    width = slabs * CAP + LANES
    chosen = ones_where(lax.broadcasted_iota(jnp.int32, (width, count), 0) == key)
    packed = sum(dot_nt(part, chosen) for part in split_3(rows_ref[...]))
    lane = lax.broadcasted_iota(jnp.int32, (8, LANES), 1)
    per_tile = LANES // CAP
    tiles = [packed[:, q * LANES:(q + 1) * LANES] for q in range(width // LANES)]
    for d in range(slabs):
        q, m = divmod(d, per_tile)
        if m == 0:
            out_ref[d] = tiles[q]
        else:
            shift = LANES - m * CAP
            out_ref[d] = jnp.where(
                lane < shift, pltpu.roll(tiles[q], shift, 1), pltpu.roll(tiles[q + 1], shift, 1)
            )


def pack(vals, target, cells, slabs):
    return pl.pallas_call(
        functools.partial(pack_kernel, slabs),
        out_shape=jax.ShapeDtypeStruct((slabs, 8, LANES), jnp.float32),
        scratch_shapes=[pltpu.VMEM((8, vals.shape[1]), jnp.float32)],
        cost_estimate=pl.CostEstimate(flops=20_000_000, bytes_accessed=100_000, transcendentals=0),
        name="pack",
    )(vals, target, cells)


def regroup(got_ref, part):
    lane = lax.broadcasted_iota(jnp.int32, (8, LANES), 1) // CAP
    per_tile = LANES // CAP
    tiles = []
    for first in range(0, got_ref.shape[0], per_tile):
        tile = None
        for j in range(per_tile):
            block = got_ref[first + j]
            shift = (j - part) * CAP % LANES
            if shift:
                block = pltpu.roll(block, shift, 1)
            tile = block if tile is None else jnp.where(lane == j, block, tile)
        tiles.append(tile)
    return jnp.concatenate(tiles, axis=1)


def split_2(value):
    high = value.astype(jnp.bfloat16).astype(jnp.float32)
    return high, value - high


def sweep_kernel(
    slab_count, factor, omega_ref, got_ref, sigma_ref, prev_hbm, fwd_hbm, up_hbm, down_hbm,
    adjoint_hbm, grad_ref,
    field_0, field_1, field_2, field_3, fwd, sig, source, coef_a, coef_b, onehot, sems,
):
    comps, width, ny, nz = field_3.shape
    wide = SWEEPS
    rim = wide - 1
    loads = [
        pltpu.make_async_copy(prev_hbm, field_0.at[:, pl.ds(wide, width)], sems.at[0]),
        pltpu.make_async_copy(fwd_hbm, fwd, sems.at[1]),
        pltpu.make_async_copy(up_hbm.at[pl.ds(0, comps)], field_0.at[:, pl.ds(0, wide)], sems.at[2]),
        pltpu.make_async_copy(down_hbm.at[pl.ds(0, comps)], field_0.at[:, pl.ds(wide + width, wide)], sems.at[3]),
        pltpu.make_async_copy(up_hbm.at[comps], sig.at[pl.ds(0, wide)], sems.at[4]),
        pltpu.make_async_copy(down_hbm.at[comps], sig.at[pl.ds(wide, wide)], sems.at[5]),
    ]
    for load in loads:
        load.start()

    own = regroup(got_ref, 1)
    count = own.shape[1]
    cell = own[6:7].astype(jnp.int32)
    row, z = cell // nz, cell % nz
    at_z = lax.broadcasted_iota(jnp.int32, (nz, count), 0) == z
    for c in range(comps):
        for half, part in enumerate(split_2(own[c:c + 1])):
            onehot[c * nz:(c + 1) * nz, half * count:(half + 1) * count] = jnp.where(at_z, part, 0.0).astype(jnp.bfloat16)
    block = 4
    for first in range(0, width, block):
        at_row = ones_where(lax.broadcasted_iota(jnp.int32, (block * ny, count), 0) + first * ny == row)
        result = dot_nt(jnp.concatenate([at_row, at_row], axis=1), onehot[...])
        for c in range(comps):
            source[c, rim + first:rim + first + block] = result[:, c * nz:(c + 1) * nz].reshape(block, ny, nz)
    for part, first, at in ((0, width - rim, 0), (2, 0, rim + width)):
        side = regroup(got_ref, part)
        cell = side[6:7].astype(jnp.int32)
        row, z = cell // nz - first * ny, cell % nz
        at_z = ones_where(lax.broadcasted_iota(jnp.int32, (nz, count), 0) == z)
        at_row = lax.broadcasted_iota(jnp.int32, (rim * ny, count), 0) == row
        for c in range(comps):
            high, low = split_2(side[c:c + 1])
            result = dot_nt(jnp.where(at_row, high, 0.0).astype(jnp.bfloat16), at_z)
            result += dot_nt(jnp.where(at_row, low, 0.0).astype(jnp.bfloat16), at_z)
            source[c, at:at + rim] = result.reshape(rim, ny, nz)

    omega = omega_ref[0]

    def coefficients(cells):
        beta = omega * cells
        inverse = 1.0 / (36.0 + beta * beta)
        return 6.0 * inverse, beta * inverse

    coef_a[rim:rim + width], coef_b[rim:rim + width] = coefficients(sigma_ref[...])
    for load in loads:
        load.wait()
    me = lax.axis_index("slab")
    for there, first, at in ((me > 0, 1, 0), (me < slab_count - 1, wide, rim + width)):
        inside = jnp.where(there, 1.0, 0.0)
        side_a, side_b = coefficients(sig[first:first + rim])
        coef_a[at:at + rim], coef_b[at:at + rim] = side_a * inside, side_b * inside

    ys = lax.broadcasted_iota(jnp.int32, (ny, nz), 0)
    zs = lax.broadcasted_iota(jnp.int32, (ny, nz), 1)
    first_y, last_y, first_z, last_z = ys == 0, ys == ny - 1, zs == 0, zs == nz - 1

    def beside(field, c, x):
        middle = field[c, x + 1]
        total = field[c, x] + field[c, x + 2]
        total += jnp.where(first_y, 0.0, pltpu.roll(middle, 1, 0)) + jnp.where(last_y, 0.0, pltpu.roll(middle, ny - 1, 0))
        total += jnp.where(first_z, 0.0, pltpu.roll(middle, 1, 1)) + jnp.where(last_z, 0.0, pltpu.roll(middle, nz - 1, 1))
        return total

    def sweep(old, new, layers, skip, last):
        def layer(x, carry):
            a, b = coef_a[x + skip], coef_b[x + skip]
            terms = jnp.zeros((ny, nz), jnp.float32)
            for c in range(comps // 2):
                d = c + comps // 2
                real = source[c, x + skip] + beside(old, c, x)
                imag = source[d, x + skip] + beside(old, d, x)
                real, imag = a * real - b * imag, a * imag + b * real
                new[c, x] = real
                new[d, x] = imag
                if last:
                    terms += fwd[c, x] * imag + fwd[d, x] * real
            if last:
                grad_ref[:, pl.ds(x, 1), :] = (terms * (omega * factor)).reshape(ny, 1, nz)
            return carry
        lax.fori_loop(0, layers, layer, 0)

    sweep(field_0, field_1, width + 4, 0, False)
    sweep(field_1, field_2, width + 2, 1, False)
    sweep(field_2, field_3, width, 2, True)
    store = pltpu.make_async_copy(field_3, adjoint_hbm, sems.at[6])
    store.start()
    store.wait()


def sweeps(omega, got, sigma, prev, fwd, up, down, slab_count, factor):
    comps, width, ny, nz = prev.shape
    f32 = jnp.float32
    count = got.shape[0] * CAP
    hbm = pl.BlockSpec(memory_space=pl.ANY)
    vmem = pl.BlockSpec(memory_space=pltpu.VMEM)
    return pl.pallas_call(
        functools.partial(sweep_kernel, slab_count, factor),
        out_shape=(
            jax.ShapeDtypeStruct(prev.shape, f32),
            jax.ShapeDtypeStruct((ny, width, nz), f32),
        ),
        in_specs=[pl.BlockSpec(memory_space=pltpu.SMEM), vmem, vmem, hbm, hbm, hbm, hbm],
        out_specs=(hbm, vmem),
        scratch_shapes=[
            pltpu.VMEM((comps, width + 6, ny, nz), f32),
            pltpu.VMEM((comps, width + 4, ny, nz), f32),
            pltpu.VMEM((comps, width + 2, ny, nz), f32),
            pltpu.VMEM((comps, width, ny, nz), f32),
            pltpu.VMEM((comps, width, ny, nz), f32),
            pltpu.VMEM((6, ny, nz), f32),
            pltpu.VMEM((comps, width + 4, ny, nz), f32),
            pltpu.VMEM((width + 4, ny, nz), f32),
            pltpu.VMEM((width + 4, ny, nz), f32),
            pltpu.VMEM((comps * nz, 2 * count), jnp.bfloat16),
            pltpu.SemaphoreType.DMA((7,)),
        ],
        compiler_params=pltpu.CompilerParams(vmem_limit_bytes=40 * 1024 * 1024),
        cost_estimate=pl.CostEstimate(flops=1_000_000_000, bytes_accessed=6_000_000, transcendentals=0),
        name="sweeps",
    )(omega, got, sigma, prev, fwd, up, down)


def shards(fwd_field, adj_prev, sigma, omega, res_vals, rec_slab, rec_cell):
    pairs, comps, width, ny, nz = adj_prev.shape
    slabs, groups = lax.axis_size("slab"), lax.axis_size("tx")
    prev, fwd = adj_prev[0], fwd_field[0]
    up = [(i, i + 1) for i in range(slabs - 1)]
    down = [(j, i) for i, j in up]
    highest = jnp.concatenate([prev[:, width - SWEEPS:], sigma[None, width - SWEEPS:]], axis=0)
    lowest = jnp.concatenate([prev[:, :SWEEPS], sigma[None, :SWEEPS]], axis=0)
    from_before = lax.ppermute(highest, "slab", up)
    from_after = lax.ppermute(lowest, "slab", down)
    send = pack(res_vals[0], rec_slab.reshape(1, -1), rec_cell, slabs)
    got = lax.all_to_all(send, "slab", split_axis=0, concat_axis=0, tiled=True)
    factor = 1.0 / (3.0 * pairs * groups) ** 0.5
    adjoint, terms = sweeps(omega, got, sigma, prev, fwd, from_before, from_after, slabs, factor)
    parts = lax.all_to_all(terms, "tx", split_axis=0, concat_axis=0, tiled=True)
    gradient = jnp.sum(parts, axis=0)[:, None, :]
    return (adjoint[None], gradient)


def solution(mesh):
    placed = (
        P("tx", None, "slab", None, None),
        P("tx", None, "slab", None, None),
        P("slab", None, None),
        P("tx"),
        P("tx", None, "slab"),
        P("tx", "slab", None),
        P("tx", "slab"),
    )
    return jax.shard_map(
        shards,
        mesh=mesh,
        in_specs=placed,
        out_specs=(P("tx", None, "slab", None, None), P("slab", "tx", None)),
        check_vma=False,
    )
```

```python
import functools

import jax
import jax.numpy as jnp
from jax import lax
from jax.experimental import pallas as pl
from jax.experimental.pallas import tpu as pltpu
from jax.sharding import PartitionSpec as P

SWEEPS = 3
CAP = 32
LANES = 128
COLUMNS = 4
NT = (((1,), (1,)), ((), ()))


def dot_nt(a, b):
    return lax.dot_general(a, b, NT, preferred_element_type=jnp.float32)


def split_3(value):
    high = value.astype(jnp.bfloat16)
    rest = value - high.astype(jnp.float32)
    middle = rest.astype(jnp.bfloat16)
    low = (rest - middle.astype(jnp.float32)).astype(jnp.bfloat16)
    return high, middle, low


def ones_where(mask):
    return jnp.where(mask, 1.0, 0.0).astype(jnp.bfloat16)


def pack_kernel(slabs, vals_ref, slab_ref, cell_ref, out_ref, rows_ref):
    count = vals_ref.shape[1]
    rows_ref[...] = jnp.zeros_like(rows_ref)
    rows_ref[0:6, :] = vals_ref[...]
    rows_ref[6:7, :] = cell_ref[...].astype(jnp.float32)
    target = slab_ref[...]
    member = ones_where(lax.broadcasted_iota(jnp.int32, (slabs, count), 0) == target)
    before = ones_where(
        lax.broadcasted_iota(jnp.int32, (count, count), 0)
        < lax.broadcasted_iota(jnp.int32, (count, count), 1)
    )
    ahead = jnp.dot(member, before, preferred_element_type=jnp.float32)
    rank = jnp.sum(ahead * member.astype(jnp.float32), axis=0, keepdims=True)
    key = (target + 1) * CAP + rank.astype(jnp.int32)
    width = slabs * CAP + LANES
    chosen = ones_where(lax.broadcasted_iota(jnp.int32, (width, count), 0) == key)
    packed = sum(dot_nt(part, chosen) for part in split_3(rows_ref[...]))
    lane = lax.broadcasted_iota(jnp.int32, (8, LANES), 1)
    per_tile = LANES // CAP
    tiles = [packed[:, q * LANES:(q + 1) * LANES] for q in range(width // LANES)]
    for d in range(slabs):
        q, m = divmod(d, per_tile)
        if m == 0:
            out_ref[d] = tiles[q]
        else:
            shift = LANES - m * CAP
            out_ref[d] = jnp.where(
                lane < shift, pltpu.roll(tiles[q], shift, 1), pltpu.roll(tiles[q + 1], shift, 1)
            )


def pack(vals, target, cells, slabs):
    return pl.pallas_call(
        functools.partial(pack_kernel, slabs),
        out_shape=jax.ShapeDtypeStruct((slabs, 8, LANES), jnp.float32),
        scratch_shapes=[pltpu.VMEM((8, vals.shape[1]), jnp.float32)],
        cost_estimate=pl.CostEstimate(flops=20_000_000, bytes_accessed=100_000, transcendentals=0),
        name="pack",
    )(vals, target, cells)


def regroup(got_ref, part):
    lane = lax.broadcasted_iota(jnp.int32, (8, LANES), 1) // CAP
    per_tile = LANES // CAP
    tiles = []
    for first in range(0, got_ref.shape[0], per_tile):
        tile = None
        for j in range(per_tile):
            block = got_ref[first + j]
            shift = (j - part) * CAP % LANES
            if shift:
                block = pltpu.roll(block, shift, 1)
            tile = block if tile is None else jnp.where(lane == j, block, tile)
        tiles.append(tile)
    return jnp.concatenate(tiles, axis=1)


def split_2(value):
    high = value.astype(jnp.bfloat16).astype(jnp.float32)
    return high, value - high


def coefficients(omega, cells):
    beta = omega * cells
    inverse = 1.0 / (36.0 + beta * beta)
    return 6.0 * inverse, beta * inverse


def neighbour_sum(ny, nz):
    ys = lax.broadcasted_iota(jnp.int32, (ny, nz), 0)
    zs = lax.broadcasted_iota(jnp.int32, (ny, nz), 1)
    first_y, last_y, first_z, last_z = ys == 0, ys == ny - 1, zs == 0, zs == nz - 1

    def beside(before, middle, after):
        total = before + after
        total += jnp.where(first_y, 0.0, pltpu.roll(middle, 1, 0)) + jnp.where(last_y, 0.0, pltpu.roll(middle, ny - 1, 0))
        total += jnp.where(first_z, 0.0, pltpu.roll(middle, 1, 1)) + jnp.where(last_z, 0.0, pltpu.roll(middle, nz - 1, 1))
        return total

    return beside


def inner_kernel(
    factor, omega_ref, got_ref, sigma_ref, prev_hbm, fwd_hbm,
    adjoint_hbm, grad_ref, field_1_hbm, field_2_hbm, source_hbm, coef_hbm,
    field_0, field_1, field_2, field_3, fwd, source, coef, onehot, sems,
):
    comps, width, ny, nz = field_0.shape
    rim = SWEEPS - 1
    load_prev = pltpu.make_async_copy(prev_hbm, field_0, sems.at[0])
    load_fwd = pltpu.make_async_copy(fwd_hbm, fwd, sems.at[1])
    load_prev.start()
    load_fwd.start()

    own = regroup(got_ref, 1)
    count = own.shape[1]
    cell = own[6:7].astype(jnp.int32)
    row, z = cell // nz, cell % nz
    at_z = lax.broadcasted_iota(jnp.int32, (nz, count), 0) == z
    for c in range(comps):
        for half, part in enumerate(split_2(own[c:c + 1])):
            onehot[c * nz:(c + 1) * nz, half * count:(half + 1) * count] = jnp.where(at_z, part, 0.0).astype(jnp.bfloat16)
    block = 4
    for first in range(0, width, block):
        at_row = ones_where(lax.broadcasted_iota(jnp.int32, (block * ny, count), 0) + first * ny == row)
        result = dot_nt(jnp.concatenate([at_row, at_row], axis=1), onehot[...])
        for c in range(comps):
            source[c, rim + first:rim + first + block] = result[:, c * nz:(c + 1) * nz].reshape(block, ny, nz)
    for part, first, at in ((0, width - rim, 0), (2, 0, rim + width)):
        side = regroup(got_ref, part)
        cell = side[6:7].astype(jnp.int32)
        row, z = cell // nz - first * ny, cell % nz
        at_z = ones_where(lax.broadcasted_iota(jnp.int32, (nz, count), 0) == z)
        at_row = lax.broadcasted_iota(jnp.int32, (rim * ny, count), 0) == row
        for c in range(comps):
            high, low = split_2(side[c:c + 1])
            result = dot_nt(jnp.where(at_row, high, 0.0).astype(jnp.bfloat16), at_z)
            result += dot_nt(jnp.where(at_row, low, 0.0).astype(jnp.bfloat16), at_z)
            source[c, at:at + rim] = result.reshape(rim, ny, nz)

    omega = omega_ref[0]
    coef[0], coef[1] = coefficients(omega, sigma_ref[...])
    beside = neighbour_sum(ny, nz)
    load_prev.wait()
    load_fwd.wait()

    def sweep(old, new, first, last):
        def layer(i, carry):
            x = i + first
            a, b = coef[0, x], coef[1, x]
            terms = jnp.zeros((ny, nz), jnp.float32)
            for c in range(comps // 2):
                d = c + comps // 2
                real = source[c, x + rim] + beside(old[c, i], old[c, i + 1], old[c, i + 2])
                imag = source[d, x + rim] + beside(old[d, i], old[d, i + 1], old[d, i + 2])
                real, imag = a * real - b * imag, a * imag + b * real
                new[c, i] = real
                new[d, i] = imag
                if last:
                    terms += fwd[c, x] * imag + fwd[d, x] * real
            if last:
                grad_ref[:, pl.ds(x, 1), :] = (terms * (omega * factor)).reshape(ny, 1, nz)
            return carry
        lax.fori_loop(0, new.shape[1], layer, 0)

    grad_ref[...] = jnp.zeros_like(grad_ref)
    sweep(field_0, field_1, 1, False)
    sweep(field_1, field_2, 2, False)
    sweep(field_2, field_3, 3, True)
    stores = [pltpu.make_async_copy(field_3, adjoint_hbm.at[:, pl.ds(3, width - 6)], sems.at[2])]
    for s in range(2):
        pairs = (
            (field_1.at[:, pl.ds(s * (width - 4), 2)], field_1_hbm.at[s]),
            (field_2.at[:, pl.ds(s * (width - 6), 2)], field_2_hbm.at[s]),
            (source.at[:, pl.ds(s * (width - 1), 5)], source_hbm.at[s]),
            (coef.at[:, pl.ds(s * (width - 3), 3)], coef_hbm.at[s]),
        )
        stores += [pltpu.make_async_copy(src, dst, sems.at[3 + 4 * s + n]) for n, (src, dst) in enumerate(pairs)]
    for store in stores:
        store.start()
    for store in stores:
        store.wait()


def inner(omega, got, sigma, prev, fwd, factor):
    comps, width, ny, nz = prev.shape
    f32 = jnp.float32
    count = got.shape[0] * CAP
    hbm = pl.BlockSpec(memory_space=pl.ANY)
    vmem = pl.BlockSpec(memory_space=pltpu.VMEM)
    cells = (ny, nz)
    return pl.pallas_call(
        functools.partial(inner_kernel, factor),
        out_shape=[jax.ShapeDtypeStruct(shape, f32) for shape in (
            prev.shape, (ny, width, nz), (2, comps, 2) + cells, (2, comps, 2) + cells, (2, comps, 5) + cells, (2, 2, 3) + cells,
        )],
        in_specs=[pl.BlockSpec(memory_space=pltpu.SMEM), vmem, vmem, hbm, hbm],
        out_specs=[hbm, vmem, hbm, hbm, hbm, hbm],
        scratch_shapes=[
            pltpu.VMEM((comps, width) + cells, f32),
            pltpu.VMEM((comps, width - 2) + cells, f32),
            pltpu.VMEM((comps, width - 4) + cells, f32),
            pltpu.VMEM((comps, width - 6) + cells, f32),
            pltpu.VMEM((comps, width) + cells, f32),
            pltpu.VMEM((comps, width + 4) + cells, f32),
            pltpu.VMEM((2, width) + cells, f32),
            pltpu.VMEM((comps * nz, 2 * count), jnp.bfloat16),
            pltpu.SemaphoreType.DMA((11,)),
        ],
        compiler_params=pltpu.CompilerParams(vmem_limit_bytes=40 * 1024 * 1024),
        cost_estimate=pl.CostEstimate(flops=10_000_000_000, bytes_accessed=30_000_000, transcendentals=0),
        name="inner",
    )(omega, got, sigma, prev, fwd)


def outer_kernel(
    slab_count, factor, omega_ref, inner_grad_ref, prev_hbm, fwd_hbm, before_hbm, after_hbm, direct_hbm, staged_hbm,
    field_1_hbm, field_2_hbm, source_hbm, coef_hbm, inner_adjoint_hbm,
    adjoint_hbm, grad_ref,
    field_0, field_1, field_2, field_3, fwd, sig, source, coef, sems, halo_sems,
):
    comps, width, ny, nz = prev_hbm.shape
    me = lax.axis_index("slab")
    column = me % COLUMNS
    loads = []
    for s in range(2):
        pairs = (
            (prev_hbm.at[:, pl.ds(s * (width - 2), 2)], field_0.at[s, :, pl.ds(3 - 3 * s, 2)]),
            (fwd_hbm.at[:, pl.ds(s * (width - 3), 3)], fwd.at[s]),
            (field_1_hbm.at[s], field_1.at[s, :, pl.ds(3 - 3 * s, 2)]),
            (field_2_hbm.at[s], field_2.at[s, :, pl.ds(3 - 3 * s, 2)]),
            (source_hbm.at[s], source.at[s]),
            (coef_hbm.at[s], coef.at[s, :, pl.ds(2 - 2 * s, 3)]),
        )
        loads += [pltpu.make_async_copy(src, dst, sems.at[6 * s + n]) for n, (src, dst) in enumerate(pairs)]
    split = direct_hbm.shape[0]
    for s, (near, far) in enumerate(((before_hbm, 0), (after_hbm, COLUMNS - 1))):
        spot = pl.ds(2 * s, 3)
        at_edge = column == far

        @pl.when(at_edge)
        def _():
            pltpu.make_async_copy(direct_hbm, field_0.at[s, pl.ds(0, split), spot], halo_sems.at[s, 0]).start()
            pltpu.make_async_copy(staged_hbm.at[pl.ds(0, comps - split)], field_0.at[s, pl.ds(split, comps - split), spot], halo_sems.at[s, 1]).start()
            pltpu.make_async_copy(staged_hbm.at[comps - split], sig.at[s], halo_sems.at[s, 2]).start()

        @pl.when(jnp.logical_not(at_edge))
        def _():
            pltpu.make_async_copy(near.at[pl.ds(0, split)], field_0.at[s, pl.ds(0, split), spot], halo_sems.at[s, 0]).start()
            pltpu.make_async_copy(near.at[pl.ds(split, comps - split)], field_0.at[s, pl.ds(split, comps - split), spot], halo_sems.at[s, 1]).start()
            pltpu.make_async_copy(near.at[comps], sig.at[s], halo_sems.at[s, 2]).start()

        loads_of_side = (
            pltpu.make_async_copy(near.at[pl.ds(0, split)], field_0.at[s, pl.ds(0, split), spot], halo_sems.at[s, 0]),
            pltpu.make_async_copy(near.at[pl.ds(split, comps - split)], field_0.at[s, pl.ds(split, comps - split), spot], halo_sems.at[s, 1]),
            pltpu.make_async_copy(near.at[comps], sig.at[s], halo_sems.at[s, 2]),
        )
        if s == 0:
            waits = list(loads_of_side)
        else:
            waits += loads_of_side
    for load in loads:
        load.start()
    grad_ref[...] = inner_grad_ref[...]
    for load in waits + loads:
        load.wait()
    omega = omega_ref[0]
    for s, there in ((0, me > 0), (1, me < slab_count - 1)):
        inside = jnp.where(there, 1.0, 0.0)
        a, b = coefficients(omega, sig[s, 1 - s:3 - s])
        coef[s, 0, 3 * s:3 * s + 2], coef[s, 1, 3 * s:3 * s + 2] = a * inside, b * inside

    beside = neighbour_sum(ny, nz)

    def sweep(old, new, number):
        def layer(k, carry):
            for s in range(2):
                at = k + (number if s == 0 else 2 - number)
                a, b = coef[s, 0, at], coef[s, 1, at]
                terms = jnp.zeros((ny, nz), jnp.float32)
                for c in range(comps // 2):
                    d = c + comps // 2
                    real = source[s, c, at] + beside(old[s, c, k], old[s, c, k + 1], old[s, c, k + 2])
                    imag = source[s, d, at] + beside(old[s, d, k], old[s, d, k + 1], old[s, d, k + 2])
                    real, imag = a * real - b * imag, a * imag + b * real
                    to = k if number == 2 else k + 2 * s
                    new[s, c, to] = real
                    new[s, d, to] = imag
                    if number == 2:
                        terms += fwd[s, c, k] * imag + fwd[s, d, k] * real
                if number == 2:
                    grad_ref[:, pl.ds(k + s * (width - 3), 1), :] = (terms * (omega * factor)).reshape(ny, 1, nz)
            return carry
        lax.fori_loop(0, 3, layer, 0)

    sweep(field_0, field_1, 0)
    sweep(field_1, field_2, 1)
    sweep(field_2, field_3, 2)
    stores = [pltpu.make_async_copy(field_3.at[s], adjoint_hbm.at[:, pl.ds(s * (width - 3), 3)], sems.at[6 * s]) for s in range(2)]
    for store in stores:
        store.start()
    for store in stores:
        store.wait()


def outer(omega, grad, prev, fwd, halos, from_inner, adjoint, slab_count, factor):
    comps, width, ny, nz = prev.shape
    f32 = jnp.float32
    hbm = pl.BlockSpec(memory_space=pl.ANY)
    vmem = pl.BlockSpec(memory_space=pltpu.VMEM)
    cells = (ny, nz)
    return pl.pallas_call(
        functools.partial(outer_kernel, slab_count, factor),
        out_shape=(jax.ShapeDtypeStruct(prev.shape, f32), jax.ShapeDtypeStruct(grad.shape, f32)),
        in_specs=[pl.BlockSpec(memory_space=pltpu.SMEM), vmem] + [hbm] * 11,
        out_specs=(hbm, vmem),
        scratch_shapes=[
            pltpu.VMEM((2, comps, 5) + cells, f32),
            pltpu.VMEM((2, comps, 5) + cells, f32),
            pltpu.VMEM((2, comps, 5) + cells, f32),
            pltpu.VMEM((2, comps, 3) + cells, f32),
            pltpu.VMEM((2, comps, 3) + cells, f32),
            pltpu.VMEM((2, 3) + cells, f32),
            pltpu.VMEM((2, comps, 5) + cells, f32),
            pltpu.VMEM((2, 2, 5) + cells, f32),
            pltpu.SemaphoreType.DMA((12,)),
            pltpu.SemaphoreType.DMA((2, 3)),
        ],
        input_output_aliases={12: 0},
        compiler_params=pltpu.CompilerParams(vmem_limit_bytes=24 * 1024 * 1024),
        cost_estimate=pl.CostEstimate(flops=100_000_000, bytes_accessed=3_000_000, transcendentals=0),
        name="outer",
    )(omega, grad, prev, fwd, *halos, *from_inner, adjoint)


def shards(fwd_field, adj_prev, sigma, omega, res_vals, rec_slab, rec_cell):
    pairs, comps, width, ny, nz = adj_prev.shape
    slabs, groups = lax.axis_size("slab"), lax.axis_size("tx")
    prev, fwd = adj_prev[0], fwd_field[0]
    ring = [(i, i + 1 if (i + 1) % COLUMNS else i + 1 - COLUMNS) for i in range(slabs)]
    crossing = [(i, i + 1) for i in range(COLUMNS - 1, slabs - 1, COLUMNS)]
    straight = [(i, i + COLUMNS) for i in range(0, slabs - COLUMNS, COLUMNS)]
    straight += [(i + COLUMNS, i) for i in range(COLUMNS - 1, slabs - COLUMNS, COLUMNS)]
    column = lax.axis_index("slab") % COLUMNS
    highest = jnp.concatenate([prev[:, width - SWEEPS:], sigma[None, width - SWEEPS:]], axis=0)
    lowest = jnp.concatenate([prev[:, :SWEEPS], sigma[None, :SWEEPS]], axis=0)
    before = lax.ppermute(highest, "slab", ring)
    after = lax.ppermute(lowest, "slab", [(j, i) for i, j in ring])
    split = 4
    direct = lax.ppermute(
        jnp.where(column == COLUMNS - 1, highest[:split], lowest[:split]), "slab", crossing + [(j, i) for i, j in crossing]
    )
    staged = lax.ppermute(jnp.where(column == 0, before[split:], after[split:]), "slab", straight)
    send = pack(res_vals[0], rec_slab.reshape(1, -1), rec_cell, slabs)
    got = lax.all_to_all(send, "slab", split_axis=0, concat_axis=0, tiled=True)
    factor = 1.0 / (3.0 * pairs * groups) ** 0.5
    adjoint, terms, *from_inner = inner(omega, got, sigma, prev, fwd, factor)
    halos = (before, after, direct, staged)
    adjoint, terms = outer(omega, terms, prev, fwd, halos, from_inner, adjoint, slabs, factor)
    parts = lax.all_to_all(terms, "tx", split_axis=0, concat_axis=0, tiled=True)
    gradient = jnp.sum(parts, axis=0)[:, None, :]
    return (adjoint[None], gradient)


def solution(mesh):
    placed = (
        P("tx", None, "slab", None, None),
        P("tx", None, "slab", None, None),
        P("slab", None, None),
        P("tx"),
        P("tx", None, "slab"),
        P("tx", "slab", None),
        P("tx", "slab"),
    )
    return jax.shard_map(
        shards,
        mesh=mesh,
        in_specs=placed,
        out_specs=(P("tx", None, "slab", None, None), P("slab", "tx", None)),
        check_vma=False,
    )
```

```python
import functools

import jax
import jax.numpy as jnp
from jax import lax
from jax.experimental import pallas as pl
from jax.experimental.pallas import tpu as pltpu
from jax.sharding import PartitionSpec as P

SWEEPS = 3
CAP = 32
LANES = 128
COLUMNS = 4
NT = (((1,), (1,)), ((), ()))


def dot_nt(a, b):
    return lax.dot_general(a, b, NT, preferred_element_type=jnp.float32)


def split_3(value):
    high = value.astype(jnp.bfloat16)
    rest = value - high.astype(jnp.float32)
    middle = rest.astype(jnp.bfloat16)
    low = (rest - middle.astype(jnp.float32)).astype(jnp.bfloat16)
    return high, middle, low


def ones_where(mask):
    return jnp.where(mask, 1.0, 0.0).astype(jnp.bfloat16)


def pack_kernel(
    slabs, vals_ref, slab_ref, cell_ref, prev_hbm, sigma_hbm,
    out_ref, highest_hbm, lowest_hbm, cross_a_hbm, cross_b_hbm, rows_ref, sems,
):
    comps, width = prev_hbm.shape[:2]
    split = cross_a_hbm.shape[0]
    last = lax.axis_index("slab") % COLUMNS == COLUMNS - 1
    upper, lower = pl.ds(width - SWEEPS, SWEEPS), pl.ds(0, SWEEPS)

    def crossing(layers):
        return [
            pltpu.make_async_copy(prev_hbm.at[pl.ds(0, split), layers], cross_a_hbm, sems.at[4]),
            pltpu.make_async_copy(
                prev_hbm.at[pl.ds(split, comps - split), layers], cross_b_hbm.at[pl.ds(0, comps - split)], sems.at[5]
            ),
            pltpu.make_async_copy(sigma_hbm.at[layers], cross_b_hbm.at[comps - split], sems.at[6]),
        ]

    whole = [
        pltpu.make_async_copy(prev_hbm.at[:, upper], highest_hbm.at[pl.ds(0, comps)], sems.at[0]),
        pltpu.make_async_copy(sigma_hbm.at[upper], highest_hbm.at[comps], sems.at[1]),
        pltpu.make_async_copy(prev_hbm.at[:, lower], lowest_hbm.at[pl.ds(0, comps)], sems.at[2]),
        pltpu.make_async_copy(sigma_hbm.at[lower], lowest_hbm.at[comps], sems.at[3]),
    ]

    @pl.when(last)
    def _():
        for copy in crossing(upper):
            copy.start()

    @pl.when(jnp.logical_not(last))
    def _():
        for copy in crossing(lower):
            copy.start()

    for copy in whole:
        copy.start()

    count = vals_ref.shape[2]
    rows_ref[...] = jnp.zeros_like(rows_ref)
    for c in range(comps):
        rows_ref[c:c + 1, :] = vals_ref[c]
    rows_ref[comps:comps + 1, :] = cell_ref[...].astype(jnp.float32)
    target = slab_ref[...]
    member = ones_where(lax.broadcasted_iota(jnp.int32, (slabs, count), 0) == target)
    earlier = ones_where(
        lax.broadcasted_iota(jnp.int32, (count, count), 0)
        < lax.broadcasted_iota(jnp.int32, (count, count), 1)
    )
    ahead = jnp.dot(member, earlier, preferred_element_type=jnp.float32)
    rank = jnp.sum(ahead * member.astype(jnp.float32), axis=0, keepdims=True)
    key = (target + 1) * CAP + rank.astype(jnp.int32)
    lanes = slabs * CAP + LANES
    chosen = ones_where(lax.broadcasted_iota(jnp.int32, (lanes, count), 0) == key)
    packed = sum(dot_nt(part, chosen) for part in split_3(rows_ref[...]))
    lane = lax.broadcasted_iota(jnp.int32, (8, LANES), 1)
    per_tile = LANES // CAP
    tiles = [packed[:, q * LANES:(q + 1) * LANES] for q in range(lanes // LANES)]
    for d in range(slabs):
        q, m = divmod(d, per_tile)
        if m == 0:
            out_ref[d] = tiles[q]
        else:
            shift = LANES - m * CAP
            out_ref[d] = jnp.where(
                lane < shift, pltpu.roll(tiles[q], shift, 1), pltpu.roll(tiles[q + 1], shift, 1)
            )
    for copy in crossing(lower) + whole:
        copy.wait()


def pack(vals, target, cells, prev, sigma, slabs, split):
    comps, _, ny, nz = prev.shape
    f32 = jnp.float32
    hbm = pl.BlockSpec(memory_space=pl.ANY)
    vmem = pl.BlockSpec(memory_space=pltpu.VMEM)
    return pl.pallas_call(
        functools.partial(pack_kernel, slabs),
        out_shape=[jax.ShapeDtypeStruct((slabs, 8, LANES), f32)] + [
            jax.ShapeDtypeStruct((blocks, SWEEPS, ny, nz), f32) for blocks in (comps + 1, comps + 1, split, comps + 1 - split)
        ],
        in_specs=[vmem, vmem, vmem, hbm, hbm],
        out_specs=[vmem, hbm, hbm, hbm, hbm],
        scratch_shapes=[pltpu.VMEM((8, vals.shape[2]), f32), pltpu.SemaphoreType.DMA((7,))],
        cost_estimate=pl.CostEstimate(flops=20_000_000, bytes_accessed=100_000, transcendentals=0),
        name="pack",
    )(vals, target, cells, prev, sigma)


def regroup(got_ref, part):
    lane = lax.broadcasted_iota(jnp.int32, (8, LANES), 1) // CAP
    per_tile = LANES // CAP
    tiles = []
    for first in range(0, got_ref.shape[0], per_tile):
        tile = None
        for j in range(per_tile):
            block = got_ref[first + j]
            shift = (j - part) * CAP % LANES
            if shift:
                block = pltpu.roll(block, shift, 1)
            tile = block if tile is None else jnp.where(lane == j, block, tile)
        tiles.append(tile)
    return jnp.concatenate(tiles, axis=1)


def split_2(value):
    high = value.astype(jnp.bfloat16).astype(jnp.float32)
    return high, value - high


def coefficients(omega, cells):
    beta = omega * cells
    inverse = 1.0 / (36.0 + beta * beta)
    return 6.0 * inverse, beta * inverse


def neighbour_sum(ny, nz):
    ys = lax.broadcasted_iota(jnp.int32, (ny, nz), 0)
    zs = lax.broadcasted_iota(jnp.int32, (ny, nz), 1)
    first_y, last_y, first_z, last_z = ys == 0, ys == ny - 1, zs == 0, zs == nz - 1

    def beside(before, middle, after):
        total = before + after
        total += jnp.where(first_y, 0.0, pltpu.roll(middle, 1, 0)) + jnp.where(last_y, 0.0, pltpu.roll(middle, ny - 1, 0))
        total += jnp.where(first_z, 0.0, pltpu.roll(middle, 1, 1)) + jnp.where(last_z, 0.0, pltpu.roll(middle, nz - 1, 1))
        return total

    return beside


def inner_kernel(
    factor, omega_ref, got_ref, sigma_ref, prev_hbm, fwd_hbm,
    adjoint_hbm, grad_ref, field_1_hbm, field_2_hbm, source_hbm, coef_hbm,
    field_0, field_1, field_2, field_3, fwd, source, coef, onehot, sems,
):
    comps, width, ny, nz = field_0.shape
    rim = SWEEPS - 1
    load_prev = pltpu.make_async_copy(prev_hbm, field_0, sems.at[0])
    load_fwd = pltpu.make_async_copy(fwd_hbm, fwd, sems.at[1])
    load_prev.start()
    load_fwd.start()

    own = regroup(got_ref, 1)
    count = own.shape[1]
    cell = own[6:7].astype(jnp.int32)
    row, z = cell // nz, cell % nz
    at_z = lax.broadcasted_iota(jnp.int32, (nz, count), 0) == z
    for c in range(comps):
        for half, part in enumerate(split_2(own[c:c + 1])):
            onehot[c * nz:(c + 1) * nz, half * count:(half + 1) * count] = jnp.where(at_z, part, 0.0).astype(jnp.bfloat16)
    block = 4
    for first in range(0, width, block):
        at_row = ones_where(lax.broadcasted_iota(jnp.int32, (block * ny, count), 0) + first * ny == row)
        result = dot_nt(jnp.concatenate([at_row, at_row], axis=1), onehot[...])
        for c in range(comps):
            source[c, rim + first:rim + first + block] = result[:, c * nz:(c + 1) * nz].reshape(block, ny, nz)
    for part, first, at in ((0, width - rim, 0), (2, 0, rim + width)):
        side = regroup(got_ref, part)
        cell = side[6:7].astype(jnp.int32)
        row, z = cell // nz - first * ny, cell % nz
        at_z = ones_where(lax.broadcasted_iota(jnp.int32, (nz, count), 0) == z)
        at_row = lax.broadcasted_iota(jnp.int32, (rim * ny, count), 0) == row
        for c in range(comps):
            high, low = split_2(side[c:c + 1])
            result = dot_nt(jnp.where(at_row, high, 0.0).astype(jnp.bfloat16), at_z)
            result += dot_nt(jnp.where(at_row, low, 0.0).astype(jnp.bfloat16), at_z)
            source[c, at:at + rim] = result.reshape(rim, ny, nz)

    omega = omega_ref[0]
    coef[0], coef[1] = coefficients(omega, sigma_ref[...])
    beside = neighbour_sum(ny, nz)
    load_prev.wait()
    load_fwd.wait()

    def sweep(old, new, first, last):
        def layer(i, carry):
            x = i + first
            a, b = coef[0, x], coef[1, x]
            terms = jnp.zeros((ny, nz), jnp.float32)
            for c in range(comps // 2):
                d = c + comps // 2
                real = source[c, x + rim] + beside(old[c, i], old[c, i + 1], old[c, i + 2])
                imag = source[d, x + rim] + beside(old[d, i], old[d, i + 1], old[d, i + 2])
                real, imag = a * real - b * imag, a * imag + b * real
                new[c, i] = real
                new[d, i] = imag
                if last:
                    terms += fwd[c, x] * imag + fwd[d, x] * real
            if last:
                grad_ref[:, pl.ds(x, 1), :] = (terms * (omega * factor)).reshape(ny, 1, nz)
            return carry
        lax.fori_loop(0, new.shape[1], layer, 0)

    grad_ref[...] = jnp.zeros_like(grad_ref)
    sweep(field_0, field_1, 1, False)
    sweep(field_1, field_2, 2, False)
    sweep(field_2, field_3, 3, True)
    stores = [pltpu.make_async_copy(field_3, adjoint_hbm.at[:, pl.ds(3, width - 6)], sems.at[2])]
    for s in range(2):
        pairs = (
            (field_1.at[:, pl.ds(s * (width - 4), 2)], field_1_hbm.at[s]),
            (field_2.at[:, pl.ds(s * (width - 6), 2)], field_2_hbm.at[s]),
            (source.at[:, pl.ds(s * (width - 1), 5)], source_hbm.at[s]),
            (coef.at[:, pl.ds(s * (width - 3), 3)], coef_hbm.at[s]),
        )
        stores += [pltpu.make_async_copy(src, dst, sems.at[3 + 4 * s + n]) for n, (src, dst) in enumerate(pairs)]
    for store in stores:
        store.start()
    for store in stores:
        store.wait()


def inner(omega, got, sigma, prev, fwd, factor):
    comps, width, ny, nz = prev.shape
    f32 = jnp.float32
    count = got.shape[0] * CAP
    hbm = pl.BlockSpec(memory_space=pl.ANY)
    vmem = pl.BlockSpec(memory_space=pltpu.VMEM)
    cells = (ny, nz)
    return pl.pallas_call(
        functools.partial(inner_kernel, factor),
        out_shape=[jax.ShapeDtypeStruct(shape, f32) for shape in (
            prev.shape, (ny, width, nz), (2, comps, 2) + cells, (2, comps, 2) + cells, (2, comps, 5) + cells, (2, 2, 3) + cells,
        )],
        in_specs=[pl.BlockSpec(memory_space=pltpu.SMEM), vmem, vmem, hbm, hbm],
        out_specs=[hbm, vmem, hbm, hbm, hbm, hbm],
        scratch_shapes=[
            pltpu.VMEM((comps, width) + cells, f32),
            pltpu.VMEM((comps, width - 2) + cells, f32),
            pltpu.VMEM((comps, width - 4) + cells, f32),
            pltpu.VMEM((comps, width - 6) + cells, f32),
            pltpu.VMEM((comps, width) + cells, f32),
            pltpu.VMEM((comps, width + 4) + cells, f32),
            pltpu.VMEM((2, width) + cells, f32),
            pltpu.VMEM((comps * nz, 2 * count), jnp.bfloat16),
            pltpu.SemaphoreType.DMA((11,)),
        ],
        compiler_params=pltpu.CompilerParams(vmem_limit_bytes=40 * 1024 * 1024),
        cost_estimate=pl.CostEstimate(flops=10_000_000_000, bytes_accessed=30_000_000, transcendentals=0),
        name="inner",
    )(omega, got, sigma, prev, fwd)


def outer_kernel(
    slab_count, factor, omega_ref, inner_grad_ref, prev_hbm, fwd_hbm, before_hbm, after_hbm, direct_hbm, staged_hbm,
    field_1_hbm, field_2_hbm, source_hbm, coef_hbm, inner_adjoint_hbm,
    adjoint_hbm, grad_ref,
    field_0, field_1, field_2, field_3, fwd, sig, source, coef, sems, halo_sems,
):
    comps, width, ny, nz = prev_hbm.shape
    me = lax.axis_index("slab")
    column = me % COLUMNS
    loads = []
    for s in range(2):
        pairs = (
            (prev_hbm.at[:, pl.ds(s * (width - 2), 2)], field_0.at[s, :, pl.ds(3 - 3 * s, 2)]),
            (fwd_hbm.at[:, pl.ds(s * (width - 3), 3)], fwd.at[s]),
            (field_1_hbm.at[s], field_1.at[s, :, pl.ds(3 - 3 * s, 2)]),
            (field_2_hbm.at[s], field_2.at[s, :, pl.ds(3 - 3 * s, 2)]),
            (source_hbm.at[s], source.at[s]),
            (coef_hbm.at[s], coef.at[s, :, pl.ds(2 - 2 * s, 3)]),
        )
        loads += [pltpu.make_async_copy(src, dst, sems.at[6 * s + n]) for n, (src, dst) in enumerate(pairs)]
    split = direct_hbm.shape[0]
    for s, (near, far) in enumerate(((before_hbm, 0), (after_hbm, COLUMNS - 1))):
        spot = pl.ds(2 * s, 3)
        at_edge = column == far

        @pl.when(at_edge)
        def _():
            pltpu.make_async_copy(direct_hbm, field_0.at[s, pl.ds(0, split), spot], halo_sems.at[s, 0]).start()
            pltpu.make_async_copy(staged_hbm.at[pl.ds(0, comps - split)], field_0.at[s, pl.ds(split, comps - split), spot], halo_sems.at[s, 1]).start()
            pltpu.make_async_copy(staged_hbm.at[comps - split], sig.at[s], halo_sems.at[s, 2]).start()

        @pl.when(jnp.logical_not(at_edge))
        def _():
            pltpu.make_async_copy(near.at[pl.ds(0, split)], field_0.at[s, pl.ds(0, split), spot], halo_sems.at[s, 0]).start()
            pltpu.make_async_copy(near.at[pl.ds(split, comps - split)], field_0.at[s, pl.ds(split, comps - split), spot], halo_sems.at[s, 1]).start()
            pltpu.make_async_copy(near.at[comps], sig.at[s], halo_sems.at[s, 2]).start()

        loads_of_side = (
            pltpu.make_async_copy(near.at[pl.ds(0, split)], field_0.at[s, pl.ds(0, split), spot], halo_sems.at[s, 0]),
            pltpu.make_async_copy(near.at[pl.ds(split, comps - split)], field_0.at[s, pl.ds(split, comps - split), spot], halo_sems.at[s, 1]),
            pltpu.make_async_copy(near.at[comps], sig.at[s], halo_sems.at[s, 2]),
        )
        if s == 0:
            waits = list(loads_of_side)
        else:
            waits += loads_of_side
    for load in loads:
        load.start()
    grad_ref[...] = inner_grad_ref[...]
    for load in waits + loads:
        load.wait()
    omega = omega_ref[0]
    for s, there in ((0, me > 0), (1, me < slab_count - 1)):
        inside = jnp.where(there, 1.0, 0.0)
        a, b = coefficients(omega, sig[s, 1 - s:3 - s])
        coef[s, 0, 3 * s:3 * s + 2], coef[s, 1, 3 * s:3 * s + 2] = a * inside, b * inside

    beside = neighbour_sum(ny, nz)

    def sweep(old, new, number):
        def layer(k, carry):
            for s in range(2):
                at = k + (number if s == 0 else 2 - number)
                a, b = coef[s, 0, at], coef[s, 1, at]
                terms = jnp.zeros((ny, nz), jnp.float32)
                for c in range(comps // 2):
                    d = c + comps // 2
                    real = source[s, c, at] + beside(old[s, c, k], old[s, c, k + 1], old[s, c, k + 2])
                    imag = source[s, d, at] + beside(old[s, d, k], old[s, d, k + 1], old[s, d, k + 2])
                    real, imag = a * real - b * imag, a * imag + b * real
                    to = k if number == 2 else k + 2 * s
                    new[s, c, to] = real
                    new[s, d, to] = imag
                    if number == 2:
                        terms += fwd[s, c, k] * imag + fwd[s, d, k] * real
                if number == 2:
                    grad_ref[:, pl.ds(k + s * (width - 3), 1), :] = (terms * (omega * factor)).reshape(ny, 1, nz)
            return carry
        lax.fori_loop(0, 3, layer, 0)

    sweep(field_0, field_1, 0)
    sweep(field_1, field_2, 1)
    sweep(field_2, field_3, 2)
    stores = [pltpu.make_async_copy(field_3.at[s], adjoint_hbm.at[:, pl.ds(s * (width - 3), 3)], sems.at[6 * s]) for s in range(2)]
    for store in stores:
        store.start()
    for store in stores:
        store.wait()


def outer(omega, grad, prev, fwd, halos, from_inner, adjoint, slab_count, factor):
    comps, width, ny, nz = prev.shape
    f32 = jnp.float32
    hbm = pl.BlockSpec(memory_space=pl.ANY)
    vmem = pl.BlockSpec(memory_space=pltpu.VMEM)
    cells = (ny, nz)
    return pl.pallas_call(
        functools.partial(outer_kernel, slab_count, factor),
        out_shape=(jax.ShapeDtypeStruct(prev.shape, f32), jax.ShapeDtypeStruct(grad.shape, f32)),
        in_specs=[pl.BlockSpec(memory_space=pltpu.SMEM), vmem] + [hbm] * 11,
        out_specs=(hbm, vmem),
        scratch_shapes=[
            pltpu.VMEM((2, comps, 5) + cells, f32),
            pltpu.VMEM((2, comps, 5) + cells, f32),
            pltpu.VMEM((2, comps, 5) + cells, f32),
            pltpu.VMEM((2, comps, 3) + cells, f32),
            pltpu.VMEM((2, comps, 3) + cells, f32),
            pltpu.VMEM((2, 3) + cells, f32),
            pltpu.VMEM((2, comps, 5) + cells, f32),
            pltpu.VMEM((2, 2, 5) + cells, f32),
            pltpu.SemaphoreType.DMA((12,)),
            pltpu.SemaphoreType.DMA((2, 3)),
        ],
        input_output_aliases={12: 0},
        compiler_params=pltpu.CompilerParams(vmem_limit_bytes=24 * 1024 * 1024),
        cost_estimate=pl.CostEstimate(flops=100_000_000, bytes_accessed=3_000_000, transcendentals=0),
        name="outer",
    )(omega, grad, prev, fwd, *halos, *from_inner, adjoint)


def shards(fwd_field, adj_prev, sigma, omega, res_vals, rec_slab, rec_cell):
    pairs, comps, width, ny, nz = adj_prev.shape
    slabs, groups = lax.axis_size("slab"), lax.axis_size("tx")
    prev, fwd = adj_prev[0], fwd_field[0]
    rows = range(0, slabs, COLUMNS)
    up = [(r + i, r + i + 1) for r in rows for i in range(COLUMNS - 1)]
    down = [(j, i) for i, j in up]
    stage_a = [(r + 3, r) for r in rows] + [(r, r + 3) for r in rows]
    stage_b = [(r + 3, r + 1) for r in rows] + [(r, r + 2) for r in rows]
    cross_a = [(r, r + COLUMNS) for r in rows[:-1]] + [(r + 3, r + 3 - COLUMNS) for r in rows[1:]]
    cross_b = [(r + 1, r + COLUMNS) for r in rows[:-1]] + [(r + 2, r + 3 - COLUMNS) for r in rows[1:]]
    vals = jnp.transpose(res_vals, (1, 0, 2))
    send, highest, lowest, part_a, part_b = pack(vals, rec_slab.reshape(1, -1), rec_cell, prev, sigma, slabs, 4)
    part_a = lax.ppermute(part_a, "slab", stage_a)
    part_b = lax.ppermute(part_b, "slab", stage_b)
    got = lax.all_to_all(send, "slab", split_axis=0, concat_axis=0, tiled=True)
    part_a = lax.ppermute(part_a, "slab", cross_a)
    part_b = lax.ppermute(part_b, "slab", cross_b)
    before = lax.ppermute(highest, "slab", up)
    after = lax.ppermute(lowest, "slab", down)
    factor = 1.0 / (3.0 * pairs * groups) ** 0.5
    adjoint, terms, *from_inner = inner(omega, got, sigma, prev, fwd, factor)
    halos = (before, after, part_a, part_b)
    adjoint, terms = outer(omega, terms, prev, fwd, halos, from_inner, adjoint, slabs, factor)
    parts = lax.all_to_all(terms, "tx", split_axis=0, concat_axis=0, tiled=True)
    gradient = jnp.sum(parts, axis=0)[:, None, :]
    return (adjoint[None], gradient)


def solution(mesh):
    placed = (
        P("tx", None, "slab", None, None),
        P("tx", None, "slab", None, None),
        P("slab", None, None),
        P("tx"),
        P("tx", None, "slab"),
        P("tx", "slab", None),
        P("tx", "slab"),
    )
    return jax.shard_map(
        shards,
        mesh=mesh,
        in_specs=placed,
        out_specs=(P("tx", None, "slab", None, None), P("slab", "tx", None)),
        check_vma=False,
    )
```

```python
import functools

import jax
import jax.numpy as jnp
from jax import lax
from jax.experimental import pallas as pl
from jax.experimental.pallas import tpu as pltpu
from jax.sharding import PartitionSpec as P

SWEEPS = 3
CAP = 32
LANES = 128
COLUMNS = 4
NT = (((1,), (1,)), ((), ()))


def dot_nt(a, b):
    return lax.dot_general(a, b, NT, preferred_element_type=jnp.float32)


def split_3(value):
    high = value.astype(jnp.bfloat16)
    rest = value - high.astype(jnp.float32)
    middle = rest.astype(jnp.bfloat16)
    low = (rest - middle.astype(jnp.float32)).astype(jnp.bfloat16)
    return high, middle, low


def ones_where(mask):
    return jnp.where(mask, 1.0, 0.0).astype(jnp.bfloat16)


def stage_kernel(prev_hbm, sigma_hbm, part_a_ref, part_b_ref, sems):
    comps, width = prev_hbm.shape[:2]
    split = part_a_ref.shape[0]
    last = lax.axis_index("slab") % COLUMNS == COLUMNS - 1

    def copies(first):
        layers = pl.ds(first, SWEEPS)
        return [
            pltpu.make_async_copy(prev_hbm.at[pl.ds(0, split), layers], part_a_ref, sems.at[0]),
            pltpu.make_async_copy(
                prev_hbm.at[pl.ds(split, comps - split), layers], part_b_ref.at[pl.ds(0, comps - split)], sems.at[1]
            ),
            pltpu.make_async_copy(sigma_hbm.at[layers], part_b_ref.at[comps - split], sems.at[2]),
        ]

    @pl.when(last)
    def _():
        for copy in copies(width - SWEEPS):
            copy.start()

    @pl.when(jnp.logical_not(last))
    def _():
        for copy in copies(0):
            copy.start()

    for copy in copies(0):
        copy.wait()


def stage(prev, sigma, split):
    comps, _, ny, nz = prev.shape
    hbm = pl.BlockSpec(memory_space=pl.ANY)
    vmem = pl.BlockSpec(memory_space=pltpu.VMEM)
    return pl.pallas_call(
        stage_kernel,
        out_shape=[jax.ShapeDtypeStruct((blocks, SWEEPS, ny, nz), jnp.float32) for blocks in (split, comps + 1 - split)],
        in_specs=[hbm, hbm],
        out_specs=[vmem, vmem],
        scratch_shapes=[pltpu.SemaphoreType.DMA((3,))],
        cost_estimate=pl.CostEstimate(flops=0, bytes_accessed=700_000, transcendentals=0),
        name="stage",
    )(prev, sigma)


def pack_kernel(
    slabs, vals_ref, slab_ref, cell_ref, prev_hbm, sigma_hbm, out_ref, highest_ref, lowest_ref, rows_ref, sems,
):
    comps, width = prev_hbm.shape[:2]
    copies = []
    for n, (first, ref) in enumerate(((width - SWEEPS, highest_ref), (0, lowest_ref))):
        layers = pl.ds(first, SWEEPS)
        copies.append(pltpu.make_async_copy(prev_hbm.at[:, layers], ref.at[pl.ds(0, comps)], sems.at[2 * n]))
        copies.append(pltpu.make_async_copy(sigma_hbm.at[layers], ref.at[comps], sems.at[2 * n + 1]))
    for copy in copies:
        copy.start()

    count = vals_ref.shape[2]
    rows_ref[...] = jnp.zeros_like(rows_ref)
    for c in range(comps):
        rows_ref[c:c + 1, :] = vals_ref[c]
    rows_ref[comps:comps + 1, :] = cell_ref[...].astype(jnp.float32)
    target = slab_ref[...]
    member = ones_where(lax.broadcasted_iota(jnp.int32, (slabs, count), 0) == target)
    earlier = ones_where(
        lax.broadcasted_iota(jnp.int32, (count, count), 0)
        < lax.broadcasted_iota(jnp.int32, (count, count), 1)
    )
    ahead = jnp.dot(member, earlier, preferred_element_type=jnp.float32)
    rank = jnp.sum(ahead * member.astype(jnp.float32), axis=0, keepdims=True)
    key = (target + 1) * CAP + rank.astype(jnp.int32)
    lanes = slabs * CAP + LANES
    chosen = ones_where(lax.broadcasted_iota(jnp.int32, (lanes, count), 0) == key)
    packed = sum(dot_nt(part, chosen) for part in split_3(rows_ref[...]))
    lane = lax.broadcasted_iota(jnp.int32, (8, LANES), 1)
    per_tile = LANES // CAP
    tiles = [packed[:, q * LANES:(q + 1) * LANES] for q in range(lanes // LANES)]
    for d in range(slabs):
        q, m = divmod(d, per_tile)
        if m == 0:
            out_ref[d] = tiles[q]
        else:
            shift = LANES - m * CAP
            out_ref[d] = jnp.where(
                lane < shift, pltpu.roll(tiles[q], shift, 1), pltpu.roll(tiles[q + 1], shift, 1)
            )
    for copy in copies:
        copy.wait()


def pack(vals, target, cells, prev, sigma, slabs):
    comps, _, ny, nz = prev.shape
    f32 = jnp.float32
    hbm = pl.BlockSpec(memory_space=pl.ANY)
    vmem = pl.BlockSpec(memory_space=pltpu.VMEM)
    return pl.pallas_call(
        functools.partial(pack_kernel, slabs),
        out_shape=[jax.ShapeDtypeStruct((slabs, 8, LANES), f32)]
        + [jax.ShapeDtypeStruct((comps + 1, SWEEPS, ny, nz), f32)] * 2,
        in_specs=[vmem, vmem, vmem, hbm, hbm],
        out_specs=[vmem, vmem, vmem],
        scratch_shapes=[pltpu.VMEM((8, vals.shape[2]), f32), pltpu.SemaphoreType.DMA((4,))],
        cost_estimate=pl.CostEstimate(flops=20_000_000, bytes_accessed=100_000, transcendentals=0),
        name="pack",
    )(vals, target, cells, prev, sigma)


def regroup(got_ref, part):
    lane = lax.broadcasted_iota(jnp.int32, (8, LANES), 1) // CAP
    per_tile = LANES // CAP
    tiles = []
    for first in range(0, got_ref.shape[0], per_tile):
        tile = None
        for j in range(per_tile):
            block = got_ref[first + j]
            shift = (j - part) * CAP % LANES
            if shift:
                block = pltpu.roll(block, shift, 1)
            tile = block if tile is None else jnp.where(lane == j, block, tile)
        tiles.append(tile)
    return jnp.concatenate(tiles, axis=1)


def split_2(value):
    high = value.astype(jnp.bfloat16).astype(jnp.float32)
    return high, value - high


def coefficients(omega, cells):
    beta = omega * cells
    inverse = 1.0 / (36.0 + beta * beta)
    return 6.0 * inverse, beta * inverse


def neighbour_sum(ny, nz):
    ys = lax.broadcasted_iota(jnp.int32, (ny, nz), 0)
    zs = lax.broadcasted_iota(jnp.int32, (ny, nz), 1)
    first_y, last_y, first_z, last_z = ys == 0, ys == ny - 1, zs == 0, zs == nz - 1

    def beside(before, middle, after):
        total = before + after
        total += jnp.where(first_y, 0.0, pltpu.roll(middle, 1, 0)) + jnp.where(last_y, 0.0, pltpu.roll(middle, ny - 1, 0))
        total += jnp.where(first_z, 0.0, pltpu.roll(middle, 1, 1)) + jnp.where(last_z, 0.0, pltpu.roll(middle, nz - 1, 1))
        return total

    return beside


def inner_kernel(
    factor, omega_ref, got_ref, sigma_hbm, prev_hbm, fwd_hbm,
    adjoint_hbm, grad_ref, field_1_hbm, field_2_hbm, source_hbm, coef_hbm,
    field_0, field_1, field_2, field_3, fwd, sig, source, coef, onehot, sems,
):
    comps, width, ny, nz = field_0.shape
    rim = SWEEPS - 1
    load_prev = pltpu.make_async_copy(prev_hbm, field_0, sems.at[0])
    load_fwd = pltpu.make_async_copy(fwd_hbm, fwd, sems.at[1])
    load_sigma = pltpu.make_async_copy(sigma_hbm, sig, sems.at[11])
    for load in (load_prev, load_sigma, load_fwd):
        load.start()

    own = regroup(got_ref, 1)
    count = own.shape[1]
    cell = own[6:7].astype(jnp.int32)
    row, z = cell // nz, cell % nz
    at_z = lax.broadcasted_iota(jnp.int32, (nz, count), 0) == z
    for c in range(comps):
        for half, part in enumerate(split_2(own[c:c + 1])):
            onehot[c * nz:(c + 1) * nz, half * count:(half + 1) * count] = jnp.where(at_z, part, 0.0).astype(jnp.bfloat16)
    block = 4
    for first in range(0, width, block):
        at_row = ones_where(lax.broadcasted_iota(jnp.int32, (block * ny, count), 0) + first * ny == row)
        result = dot_nt(jnp.concatenate([at_row, at_row], axis=1), onehot[...])
        for c in range(comps):
            source[c, rim + first:rim + first + block] = result[:, c * nz:(c + 1) * nz].reshape(block, ny, nz)
    for part, first, at in ((0, width - rim, 0), (2, 0, rim + width)):
        side = regroup(got_ref, part)
        cell = side[6:7].astype(jnp.int32)
        row, z = cell // nz - first * ny, cell % nz
        at_z = ones_where(lax.broadcasted_iota(jnp.int32, (nz, count), 0) == z)
        at_row = lax.broadcasted_iota(jnp.int32, (rim * ny, count), 0) == row
        for c in range(comps):
            high, low = split_2(side[c:c + 1])
            result = dot_nt(jnp.where(at_row, high, 0.0).astype(jnp.bfloat16), at_z)
            result += dot_nt(jnp.where(at_row, low, 0.0).astype(jnp.bfloat16), at_z)
            source[c, at:at + rim] = result.reshape(rim, ny, nz)

    omega = omega_ref[0]
    load_sigma.wait()
    coef[0], coef[1] = coefficients(omega, sig[...])
    beside = neighbour_sum(ny, nz)
    load_prev.wait()

    def sweep(old, new, first, last):
        def layer(i, carry):
            x = i + first
            a, b = coef[0, x], coef[1, x]
            terms = jnp.zeros((ny, nz), jnp.float32)
            for c in range(comps // 2):
                d = c + comps // 2
                real = source[c, x + rim] + beside(old[c, i], old[c, i + 1], old[c, i + 2])
                imag = source[d, x + rim] + beside(old[d, i], old[d, i + 1], old[d, i + 2])
                real, imag = a * real - b * imag, a * imag + b * real
                new[c, i] = real
                new[d, i] = imag
                if last:
                    terms += fwd[c, x] * imag + fwd[d, x] * real
            if last:
                grad_ref[:, pl.ds(x, 1), :] = (terms * (omega * factor)).reshape(ny, 1, nz)
            return carry
        lax.fori_loop(0, new.shape[1], layer, 0, unroll=new.shape[1] // 2)

    grad_ref[...] = jnp.zeros_like(grad_ref)
    sweep(field_0, field_1, 1, False)
    sweep(field_1, field_2, 2, False)
    load_fwd.wait()
    sweep(field_2, field_3, 3, True)
    stores = [pltpu.make_async_copy(field_3, adjoint_hbm.at[:, pl.ds(3, width - 6)], sems.at[2])]
    for s in range(2):
        pairs = (
            (field_1.at[:, pl.ds(s * (width - 4), 2)], field_1_hbm.at[s]),
            (field_2.at[:, pl.ds(s * (width - 6), 2)], field_2_hbm.at[s]),
            (source.at[:, pl.ds(s * (width - 1), 5)], source_hbm.at[s]),
            (coef.at[:, pl.ds(s * (width - 3), 3)], coef_hbm.at[s]),
        )
        stores += [pltpu.make_async_copy(src, dst, sems.at[3 + 4 * s + n]) for n, (src, dst) in enumerate(pairs)]
    for store in stores:
        store.start()
    for store in stores:
        store.wait()


def inner(omega, got, sigma, prev, fwd, factor):
    comps, width, ny, nz = prev.shape
    f32 = jnp.float32
    count = got.shape[0] * CAP
    hbm = pl.BlockSpec(memory_space=pl.ANY)
    vmem = pl.BlockSpec(memory_space=pltpu.VMEM)
    cells = (ny, nz)
    return pl.pallas_call(
        functools.partial(inner_kernel, factor),
        out_shape=[jax.ShapeDtypeStruct(shape, f32) for shape in (
            prev.shape, (ny, width, nz), (2, comps, 2) + cells, (2, comps, 2) + cells, (2, comps, 5) + cells, (2, 2, 3) + cells,
        )],
        in_specs=[pl.BlockSpec(memory_space=pltpu.SMEM), vmem, hbm, hbm, hbm],
        out_specs=[hbm, vmem, hbm, hbm, hbm, hbm],
        scratch_shapes=[
            pltpu.VMEM((comps, width) + cells, f32),
            pltpu.VMEM((comps, width - 2) + cells, f32),
            pltpu.VMEM((comps, width - 4) + cells, f32),
            pltpu.VMEM((comps, width - 6) + cells, f32),
            pltpu.VMEM((comps, width) + cells, f32),
            pltpu.VMEM((width,) + cells, f32),
            pltpu.VMEM((comps, width + 4) + cells, f32),
            pltpu.VMEM((2, width) + cells, f32),
            pltpu.VMEM((comps * nz, 2 * count), jnp.bfloat16),
            pltpu.SemaphoreType.DMA((12,)),
        ],
        compiler_params=pltpu.CompilerParams(vmem_limit_bytes=40 * 1024 * 1024),
        cost_estimate=pl.CostEstimate(flops=10_000_000_000, bytes_accessed=30_000_000, transcendentals=0),
        name="inner",
    )(omega, got, sigma, prev, fwd)


def outer_kernel(
    slab_count, factor, omega_ref, inner_grad_ref, prev_hbm, fwd_hbm, before_hbm, after_hbm, direct_hbm, staged_hbm,
    field_1_hbm, field_2_hbm, source_hbm, coef_hbm, inner_adjoint_hbm,
    adjoint_hbm, grad_ref,
    field_0, field_1, field_2, field_3, fwd, sig, source, coef, sems, halo_sems,
):
    comps, width, ny, nz = prev_hbm.shape
    me = lax.axis_index("slab")
    column = me % COLUMNS
    loads = []
    for s in range(2):
        pairs = (
            (prev_hbm.at[:, pl.ds(s * (width - 2), 2)], field_0.at[s, :, pl.ds(3 - 3 * s, 2)]),
            (fwd_hbm.at[:, pl.ds(s * (width - 3), 3)], fwd.at[s]),
            (field_1_hbm.at[s], field_1.at[s, :, pl.ds(3 - 3 * s, 2)]),
            (field_2_hbm.at[s], field_2.at[s, :, pl.ds(3 - 3 * s, 2)]),
            (source_hbm.at[s], source.at[s]),
            (coef_hbm.at[s], coef.at[s, :, pl.ds(2 - 2 * s, 3)]),
        )
        loads += [pltpu.make_async_copy(src, dst, sems.at[6 * s + n]) for n, (src, dst) in enumerate(pairs)]
    split = direct_hbm.shape[0]
    for s, (near, far) in enumerate(((before_hbm, 0), (after_hbm, COLUMNS - 1))):
        spot = pl.ds(2 * s, 3)
        at_edge = column == far

        @pl.when(at_edge)
        def _():
            pltpu.make_async_copy(direct_hbm, field_0.at[s, pl.ds(0, split), spot], halo_sems.at[s, 0]).start()
            pltpu.make_async_copy(staged_hbm.at[pl.ds(0, comps - split)], field_0.at[s, pl.ds(split, comps - split), spot], halo_sems.at[s, 1]).start()
            pltpu.make_async_copy(staged_hbm.at[comps - split], sig.at[s], halo_sems.at[s, 2]).start()

        @pl.when(jnp.logical_not(at_edge))
        def _():
            pltpu.make_async_copy(near.at[pl.ds(0, split)], field_0.at[s, pl.ds(0, split), spot], halo_sems.at[s, 0]).start()
            pltpu.make_async_copy(near.at[pl.ds(split, comps - split)], field_0.at[s, pl.ds(split, comps - split), spot], halo_sems.at[s, 1]).start()
            pltpu.make_async_copy(near.at[comps], sig.at[s], halo_sems.at[s, 2]).start()

        loads_of_side = (
            pltpu.make_async_copy(near.at[pl.ds(0, split)], field_0.at[s, pl.ds(0, split), spot], halo_sems.at[s, 0]),
            pltpu.make_async_copy(near.at[pl.ds(split, comps - split)], field_0.at[s, pl.ds(split, comps - split), spot], halo_sems.at[s, 1]),
            pltpu.make_async_copy(near.at[comps], sig.at[s], halo_sems.at[s, 2]),
        )
        if s == 0:
            waits = list(loads_of_side)
        else:
            waits += loads_of_side
    for load in loads:
        load.start()
    grad_ref[...] = inner_grad_ref[...]
    for load in waits + loads:
        load.wait()
    omega = omega_ref[0]
    for s, there in ((0, me > 0), (1, me < slab_count - 1)):
        inside = jnp.where(there, 1.0, 0.0)
        a, b = coefficients(omega, sig[s, 1 - s:3 - s])
        coef[s, 0, 3 * s:3 * s + 2], coef[s, 1, 3 * s:3 * s + 2] = a * inside, b * inside

    beside = neighbour_sum(ny, nz)

    def sweep(old, new, number):
        def layer(k, carry):
            for s in range(2):
                at = k + (number if s == 0 else 2 - number)
                a, b = coef[s, 0, at], coef[s, 1, at]
                terms = jnp.zeros((ny, nz), jnp.float32)
                for c in range(comps // 2):
                    d = c + comps // 2
                    real = source[s, c, at] + beside(old[s, c, k], old[s, c, k + 1], old[s, c, k + 2])
                    imag = source[s, d, at] + beside(old[s, d, k], old[s, d, k + 1], old[s, d, k + 2])
                    real, imag = a * real - b * imag, a * imag + b * real
                    to = k if number == 2 else k + 2 * s
                    new[s, c, to] = real
                    new[s, d, to] = imag
                    if number == 2:
                        terms += fwd[s, c, k] * imag + fwd[s, d, k] * real
                if number == 2:
                    grad_ref[:, pl.ds(k + s * (width - 3), 1), :] = (terms * (omega * factor)).reshape(ny, 1, nz)
            return carry
        lax.fori_loop(0, 3, layer, 0, unroll=3)

    sweep(field_0, field_1, 0)
    sweep(field_1, field_2, 1)
    sweep(field_2, field_3, 2)
    stores = [pltpu.make_async_copy(field_3.at[s], adjoint_hbm.at[:, pl.ds(s * (width - 3), 3)], sems.at[6 * s]) for s in range(2)]
    for store in stores:
        store.start()
    for store in stores:
        store.wait()


def outer(omega, grad, prev, fwd, halos, from_inner, adjoint, slab_count, factor):
    comps, width, ny, nz = prev.shape
    f32 = jnp.float32
    hbm = pl.BlockSpec(memory_space=pl.ANY)
    vmem = pl.BlockSpec(memory_space=pltpu.VMEM)
    cells = (ny, nz)
    return pl.pallas_call(
        functools.partial(outer_kernel, slab_count, factor),
        out_shape=(jax.ShapeDtypeStruct(prev.shape, f32), jax.ShapeDtypeStruct(grad.shape, f32)),
        in_specs=[pl.BlockSpec(memory_space=pltpu.SMEM), vmem] + [hbm] * 11,
        out_specs=(hbm, vmem),
        scratch_shapes=[
            pltpu.VMEM((2, comps, 5) + cells, f32),
            pltpu.VMEM((2, comps, 5) + cells, f32),
            pltpu.VMEM((2, comps, 5) + cells, f32),
            pltpu.VMEM((2, comps, 3) + cells, f32),
            pltpu.VMEM((2, comps, 3) + cells, f32),
            pltpu.VMEM((2, 3) + cells, f32),
            pltpu.VMEM((2, comps, 5) + cells, f32),
            pltpu.VMEM((2, 2, 5) + cells, f32),
            pltpu.SemaphoreType.DMA((12,)),
            pltpu.SemaphoreType.DMA((2, 3)),
        ],
        input_output_aliases={12: 0},
        compiler_params=pltpu.CompilerParams(vmem_limit_bytes=24 * 1024 * 1024),
        cost_estimate=pl.CostEstimate(flops=100_000_000, bytes_accessed=3_000_000, transcendentals=0),
        name="outer",
    )(omega, grad, prev, fwd, *halos, *from_inner, adjoint)


def shards(fwd_field, adj_prev, sigma, omega, res_vals, rec_slab, rec_cell):
    pairs, comps, width, ny, nz = adj_prev.shape
    slabs, groups = lax.axis_size("slab"), lax.axis_size("tx")
    prev, fwd = adj_prev[0], fwd_field[0]
    rows = range(0, slabs, COLUMNS)
    up = [(r + i, r + i + 1) for r in rows for i in range(COLUMNS - 1)]
    down = [(j, i) for i, j in up]
    stage_a = [(r + 3, r) for r in rows] + [(r, r + 3) for r in rows]
    stage_b = [(r + 3, r + 1) for r in rows] + [(r, r + 2) for r in rows]
    cross_a = [(r, r + COLUMNS) for r in rows[:-1]] + [(r + 3, r + 3 - COLUMNS) for r in rows[1:]]
    cross_b = [(r + 1, r + COLUMNS) for r in rows[:-1]] + [(r + 2, r + 3 - COLUMNS) for r in rows[1:]]
    vals = jnp.transpose(res_vals, (1, 0, 2))
    part_a, part_b = stage(prev, sigma, 4)
    part_a = lax.ppermute(part_a, "slab", stage_a)
    part_b = lax.ppermute(part_b, "slab", stage_b)
    send, highest, lowest = pack(vals, rec_slab.reshape(1, -1), rec_cell, prev, sigma, slabs)
    got = lax.all_to_all(send, "slab", split_axis=0, concat_axis=0, tiled=True)
    edge = (lax.axis_index("slab") % COLUMNS) % (COLUMNS - 1) == 0
    part_a = jnp.where(edge, part_a, 0.0)
    part_a, highest, lowest = lax.optimization_barrier((part_a, highest, lowest))
    part_a = lax.ppermute(part_a, "slab", cross_a)
    part_b = lax.ppermute(part_b, "slab", cross_b)
    before = lax.ppermute(highest, "slab", up)
    after = lax.ppermute(lowest, "slab", down)
    factor = 1.0 / (3.0 * pairs * groups) ** 0.5
    adjoint, terms, *from_inner = inner(omega, got, sigma, prev, fwd, factor)
    halos = (before, after, part_a, part_b)
    adjoint, terms = outer(omega, terms, prev, fwd, halos, from_inner, adjoint, slabs, factor)
    parts = lax.all_to_all(terms, "tx", split_axis=0, concat_axis=0, tiled=True)
    gradient = jnp.sum(parts, axis=0)[:, None, :]
    return (adjoint[None], gradient)


def solution(mesh):
    placed = (
        P("tx", None, "slab", None, None),
        P("tx", None, "slab", None, None),
        P("slab", None, None),
        P("tx"),
        P("tx", None, "slab"),
        P("tx", "slab", None),
        P("tx", "slab"),
    )
    return jax.shard_map(
        shards,
        mesh=mesh,
        in_specs=placed,
        out_specs=(P("tx", None, "slab", None, None), P("slab", "tx", None)),
        check_vma=False,
    )
```

```python
import functools

import jax
import jax.numpy as jnp
from jax import lax
from jax.experimental import pallas as pl
from jax.experimental.pallas import tpu as pltpu
from jax.sharding import PartitionSpec as P

SWEEPS = 3
CAP = 32
LANES = 128
CORES = 2
COLUMNS = 4
NT = (((1,), (1,)), ((), ()))


def dot_nt(a, b):
    return lax.dot_general(a, b, NT, preferred_element_type=jnp.float32)


def split_3(value):
    high = value.astype(jnp.bfloat16)
    rest = value - high.astype(jnp.float32)
    middle = rest.astype(jnp.bfloat16)
    low = (rest - middle.astype(jnp.float32)).astype(jnp.bfloat16)
    return high, middle, low


def ones_where(mask):
    return jnp.where(mask, 1.0, 0.0).astype(jnp.bfloat16)


def pack_kernel(
    slabs, vals_ref, slab_ref, cell_ref, prev_hbm, sigma_hbm,
    out_ref, part_a_ref, part_b_ref, highest_ref, lowest_ref, rows_ref, sems,
):
    comps, width = prev_hbm.shape[:2]
    copies = []
    for n, (first, ref) in enumerate(((width - SWEEPS, highest_ref), (0, lowest_ref))):
        layers = pl.ds(first, SWEEPS)
        copies.append(pltpu.make_async_copy(prev_hbm.at[:, layers], ref.at[pl.ds(0, comps)], sems.at[2 * n]))
        copies.append(pltpu.make_async_copy(sigma_hbm.at[layers], ref.at[comps], sems.at[2 * n + 1]))
    split = part_a_ref.shape[0]
    last = lax.axis_index("slab") % COLUMNS == COLUMNS - 1

    def parts(first):
        layers = pl.ds(first, SWEEPS)
        return [
            pltpu.make_async_copy(prev_hbm.at[pl.ds(0, split), layers], part_a_ref, sems.at[4]),
            pltpu.make_async_copy(
                prev_hbm.at[pl.ds(split, comps - split), layers], part_b_ref.at[pl.ds(0, comps - split)], sems.at[5]
            ),
            pltpu.make_async_copy(sigma_hbm.at[layers], part_b_ref.at[comps - split], sems.at[6]),
        ]

    @pl.when(last)
    def _():
        for copy in parts(width - SWEEPS):
            copy.start()

    @pl.when(jnp.logical_not(last))
    def _():
        for copy in parts(0):
            copy.start()

    for copy in copies:
        copy.start()

    count = vals_ref.shape[2]
    rows_ref[...] = jnp.zeros_like(rows_ref)
    for c in range(comps):
        rows_ref[c:c + 1, :] = vals_ref[c]
    rows_ref[comps:comps + 1, :] = cell_ref[...].astype(jnp.float32)
    target = slab_ref[...]
    member = ones_where(lax.broadcasted_iota(jnp.int32, (slabs, count), 0) == target)
    earlier = ones_where(
        lax.broadcasted_iota(jnp.int32, (count, count), 0)
        < lax.broadcasted_iota(jnp.int32, (count, count), 1)
    )
    ahead = jnp.dot(member, earlier, preferred_element_type=jnp.float32)
    rank = jnp.sum(ahead * member.astype(jnp.float32), axis=0, keepdims=True)
    key = (target + 1) * CAP + rank.astype(jnp.int32)
    lanes = slabs * CAP + LANES
    chosen = ones_where(lax.broadcasted_iota(jnp.int32, (lanes, count), 0) == key)
    packed = sum(dot_nt(part, chosen) for part in split_3(rows_ref[...]))
    lane = lax.broadcasted_iota(jnp.int32, (8, LANES), 1)
    per_tile = LANES // CAP
    tiles = [packed[:, q * LANES:(q + 1) * LANES] for q in range(lanes // LANES)]
    for d in range(slabs):
        q, m = divmod(d, per_tile)
        if m == 0:
            out_ref[d] = tiles[q]
        else:
            shift = LANES - m * CAP
            out_ref[d] = jnp.where(
                lane < shift, pltpu.roll(tiles[q], shift, 1), pltpu.roll(tiles[q + 1], shift, 1)
            )
    for copy in parts(0) + copies:
        copy.wait()


def pack(vals, target, cells, prev, sigma, slabs, split):
    comps, _, ny, nz = prev.shape
    f32 = jnp.float32
    hbm = pl.BlockSpec(memory_space=pl.ANY)
    vmem = pl.BlockSpec(memory_space=pltpu.VMEM)
    return pl.pallas_call(
        functools.partial(pack_kernel, slabs),
        out_shape=[jax.ShapeDtypeStruct((slabs, 8, LANES), f32)]
        + [
            jax.ShapeDtypeStruct((blocks, SWEEPS, ny, nz), f32)
            for blocks in (split, comps + 1 - split, comps + 1, comps + 1)
        ],
        in_specs=[vmem, vmem, vmem, hbm, hbm],
        out_specs=[vmem] * 5,
        scratch_shapes=[pltpu.VMEM((8, vals.shape[2]), f32), pltpu.SemaphoreType.DMA((7,))],
        cost_estimate=pl.CostEstimate(flops=20_000_000, bytes_accessed=100_000, transcendentals=0),
        name="pack",
    )(vals, target, cells, prev, sigma)


def regroup(got_ref, part):
    lane = lax.broadcasted_iota(jnp.int32, (8, LANES), 1) // CAP
    per_tile = LANES // CAP
    tiles = []
    for first in range(0, got_ref.shape[0], per_tile):
        tile = None
        for j in range(per_tile):
            block = got_ref[first + j]
            shift = (j - part) * CAP % LANES
            if shift:
                block = pltpu.roll(block, shift, 1)
            tile = block if tile is None else jnp.where(lane == j, block, tile)
        tiles.append(tile)
    return jnp.concatenate(tiles, axis=1)


def split_2(value):
    high = value.astype(jnp.bfloat16).astype(jnp.float32)
    return high, value - high


def coefficients(omega, cells):
    beta = omega * cells
    inverse = 1.0 / (36.0 + beta * beta)
    return 6.0 * inverse, beta * inverse


def neighbour_sum(ny, nz):
    ys = lax.broadcasted_iota(jnp.int32, (ny, nz), 0)
    zs = lax.broadcasted_iota(jnp.int32, (ny, nz), 1)
    first_y, last_y, first_z, last_z = ys == 0, ys == ny - 1, zs == 0, zs == nz - 1

    def beside(before, middle, after):
        total = before + after
        total += jnp.where(first_y, 0.0, pltpu.roll(middle, 1, 0)) + jnp.where(last_y, 0.0, pltpu.roll(middle, ny - 1, 0))
        total += jnp.where(first_z, 0.0, pltpu.roll(middle, 1, 1)) + jnp.where(last_z, 0.0, pltpu.roll(middle, nz - 1, 1))
        return total

    return beside


def inner_kernel(
    factor, omega_ref, got_ref, sigma_hbm, prev_hbm, fwd_hbm,
    adjoint_hbm, grad_ref, field_1_hbm, field_2_hbm, source_hbm, coef_hbm,
    field_0, field_1, field_2, field_3, fwd, sig, source, coef, onehot, sems,
):
    comps, width, ny, nz = field_0.shape
    rim = SWEEPS - 1
    load_prev = pltpu.make_async_copy(prev_hbm, field_0, sems.at[0])
    load_fwd = pltpu.make_async_copy(fwd_hbm, fwd, sems.at[1])
    load_sigma = pltpu.make_async_copy(sigma_hbm, sig, sems.at[11])
    for load in (load_prev, load_sigma, load_fwd):
        load.start()

    own = regroup(got_ref, 1)
    count = own.shape[1]
    cell = own[6:7].astype(jnp.int32)
    row, z = cell // nz, cell % nz
    at_z = lax.broadcasted_iota(jnp.int32, (nz, count), 0) == z
    for c in range(comps):
        for half, part in enumerate(split_2(own[c:c + 1])):
            onehot[c * nz:(c + 1) * nz, half * count:(half + 1) * count] = jnp.where(at_z, part, 0.0).astype(jnp.bfloat16)
    block = 4
    for first in range(0, width, block):
        at_row = ones_where(lax.broadcasted_iota(jnp.int32, (block * ny, count), 0) + first * ny == row)
        result = dot_nt(jnp.concatenate([at_row, at_row], axis=1), onehot[...])
        for c in range(comps):
            source[c, rim + first:rim + first + block] = result[:, c * nz:(c + 1) * nz].reshape(block, ny, nz)
    for part, first, at in ((0, width - rim, 0), (2, 0, rim + width)):
        side = regroup(got_ref, part)
        cell = side[6:7].astype(jnp.int32)
        row, z = cell // nz - first * ny, cell % nz
        at_z = ones_where(lax.broadcasted_iota(jnp.int32, (nz, count), 0) == z)
        at_row = lax.broadcasted_iota(jnp.int32, (rim * ny, count), 0) == row
        for c in range(comps):
            high, low = split_2(side[c:c + 1])
            result = dot_nt(jnp.where(at_row, high, 0.0).astype(jnp.bfloat16), at_z)
            result += dot_nt(jnp.where(at_row, low, 0.0).astype(jnp.bfloat16), at_z)
            source[c, at:at + rim] = result.reshape(rim, ny, nz)

    omega = omega_ref[0]
    load_sigma.wait()
    coef[0], coef[1] = coefficients(omega, sig[...])
    beside = neighbour_sum(ny, nz)
    load_prev.wait()

    def sweep(old, new, first, last):
        def layer(i, carry):
            x = i + first
            a, b = coef[0, x], coef[1, x]
            terms = jnp.zeros((ny, nz), jnp.float32)
            for c in range(comps // 2):
                d = c + comps // 2
                real = source[c, x + rim] + beside(old[c, i], old[c, i + 1], old[c, i + 2])
                imag = source[d, x + rim] + beside(old[d, i], old[d, i + 1], old[d, i + 2])
                real, imag = a * real - b * imag, a * imag + b * real
                new[c, i] = real
                new[d, i] = imag
                if last:
                    terms += fwd[c, x] * imag + fwd[d, x] * real
            if last:
                grad_ref[:, pl.ds(x, 1), :] = (terms * (omega * factor)).reshape(ny, 1, nz)
            return carry
        lax.fori_loop(0, new.shape[1], layer, 0, unroll=new.shape[1] // 2)

    grad_ref[...] = jnp.zeros_like(grad_ref)
    sweep(field_0, field_1, 1, False)
    sweep(field_1, field_2, 2, False)
    load_fwd.wait()
    sweep(field_2, field_3, 3, True)
    stores = [pltpu.make_async_copy(field_3, adjoint_hbm.at[:, pl.ds(3, width - 6)], sems.at[2])]
    for s in range(2):
        pairs = (
            (field_1.at[:, pl.ds(s * (width - 4), 2)], field_1_hbm.at[s]),
            (field_2.at[:, pl.ds(s * (width - 6), 2)], field_2_hbm.at[s]),
            (source.at[:, pl.ds(s * (width - 1), 5)], source_hbm.at[s]),
            (coef.at[:, pl.ds(s * (width - 3), 3)], coef_hbm.at[s]),
        )
        stores += [pltpu.make_async_copy(src, dst, sems.at[3 + 4 * s + n]) for n, (src, dst) in enumerate(pairs)]
    for store in stores:
        store.start()
    for store in stores:
        store.wait()


def inner(omega, got, sigma, prev, fwd, factor):
    comps, width, ny, nz = prev.shape
    f32 = jnp.float32
    count = got.shape[0] * CAP
    hbm = pl.BlockSpec(memory_space=pl.ANY)
    vmem = pl.BlockSpec(memory_space=pltpu.VMEM)
    cells = (ny, nz)
    return pl.pallas_call(
        functools.partial(inner_kernel, factor),
        out_shape=[jax.ShapeDtypeStruct(shape, f32) for shape in (
            prev.shape, (ny, width, nz), (2, comps, 2) + cells, (2, comps, 2) + cells, (2, comps, 5) + cells, (2, 2, 3) + cells,
        )],
        in_specs=[pl.BlockSpec(memory_space=pltpu.SMEM), vmem, hbm, hbm, hbm],
        out_specs=[hbm, vmem, hbm, hbm, hbm, hbm],
        scratch_shapes=[
            pltpu.VMEM((comps, width) + cells, f32),
            pltpu.VMEM((comps, width - 2) + cells, f32),
            pltpu.VMEM((comps, width - 4) + cells, f32),
            pltpu.VMEM((comps, width - 6) + cells, f32),
            pltpu.VMEM((comps, width) + cells, f32),
            pltpu.VMEM((width,) + cells, f32),
            pltpu.VMEM((comps, width + 4) + cells, f32),
            pltpu.VMEM((2, width) + cells, f32),
            pltpu.VMEM((comps * nz, 2 * count), jnp.bfloat16),
            pltpu.SemaphoreType.DMA((12,)),
        ],
        compiler_params=pltpu.CompilerParams(vmem_limit_bytes=20 * 1024 * 1024),
        cost_estimate=pl.CostEstimate(flops=10_000_000_000, bytes_accessed=30_000_000, transcendentals=0),
        name="inner",
    )(omega, got, sigma, prev, fwd)


def outer_kernel(
    slab_count, factor, omega_ref, inner_grad_ref, prev_hbm, fwd_hbm, before_hbm, after_hbm, direct_hbm, staged_hbm,
    field_1_hbm, field_2_hbm, source_hbm, coef_hbm, inner_adjoint_hbm,
    adjoint_hbm, keep_ref, give_ref,
    field_0, field_1, field_2, field_3, fwd, sig, source, coef, grad_ref, sems, halo_sems,
):
    comps, width, ny, nz = prev_hbm.shape
    me = lax.axis_index("slab")
    column = me % COLUMNS
    loads = []
    for s in range(2):
        pairs = (
            (prev_hbm.at[:, pl.ds(s * (width - 2), 2)], field_0.at[s, :, pl.ds(3 - 3 * s, 2)]),
            (fwd_hbm.at[:, pl.ds(s * (width - 3), 3)], fwd.at[s]),
            (field_1_hbm.at[s], field_1.at[s, :, pl.ds(3 - 3 * s, 2)]),
            (field_2_hbm.at[s], field_2.at[s, :, pl.ds(3 - 3 * s, 2)]),
            (source_hbm.at[s], source.at[s]),
            (coef_hbm.at[s], coef.at[s, :, pl.ds(2 - 2 * s, 3)]),
        )
        loads += [pltpu.make_async_copy(src, dst, sems.at[6 * s + n]) for n, (src, dst) in enumerate(pairs)]
    split = direct_hbm.shape[0]
    for s, (near, far) in enumerate(((before_hbm, 0), (after_hbm, COLUMNS - 1))):
        spot = pl.ds(2 * s, 3)
        at_edge = column == far

        @pl.when(at_edge)
        def _():
            pltpu.make_async_copy(direct_hbm, field_0.at[s, pl.ds(0, split), spot], halo_sems.at[s, 0]).start()
            pltpu.make_async_copy(staged_hbm.at[pl.ds(0, comps - split)], field_0.at[s, pl.ds(split, comps - split), spot], halo_sems.at[s, 1]).start()
            pltpu.make_async_copy(staged_hbm.at[comps - split], sig.at[s], halo_sems.at[s, 2]).start()

        @pl.when(jnp.logical_not(at_edge))
        def _():
            pltpu.make_async_copy(near.at[pl.ds(0, split)], field_0.at[s, pl.ds(0, split), spot], halo_sems.at[s, 0]).start()
            pltpu.make_async_copy(near.at[pl.ds(split, comps - split)], field_0.at[s, pl.ds(split, comps - split), spot], halo_sems.at[s, 1]).start()
            pltpu.make_async_copy(near.at[comps], sig.at[s], halo_sems.at[s, 2]).start()

        loads_of_side = (
            pltpu.make_async_copy(near.at[pl.ds(0, split)], field_0.at[s, pl.ds(0, split), spot], halo_sems.at[s, 0]),
            pltpu.make_async_copy(near.at[pl.ds(split, comps - split)], field_0.at[s, pl.ds(split, comps - split), spot], halo_sems.at[s, 1]),
            pltpu.make_async_copy(near.at[comps], sig.at[s], halo_sems.at[s, 2]),
        )
        if s == 0:
            waits = list(loads_of_side)
        else:
            waits += loads_of_side
    for load in loads:
        load.start()
    grad_ref[...] = inner_grad_ref[...]
    for load in waits + loads:
        load.wait()
    omega = omega_ref[0]
    for s, there in ((0, me > 0), (1, me < slab_count - 1)):
        inside = jnp.where(there, 1.0, 0.0)
        a, b = coefficients(omega, sig[s, 1 - s:3 - s])
        coef[s, 0, 3 * s:3 * s + 2], coef[s, 1, 3 * s:3 * s + 2] = a * inside, b * inside

    beside = neighbour_sum(ny, nz)

    def sweep(old, new, number):
        def layer(k, carry):
            for s in range(2):
                at = k + (number if s == 0 else 2 - number)
                a, b = coef[s, 0, at], coef[s, 1, at]
                terms = jnp.zeros((ny, nz), jnp.float32)
                for c in range(comps // 2):
                    d = c + comps // 2
                    real = source[s, c, at] + beside(old[s, c, k], old[s, c, k + 1], old[s, c, k + 2])
                    imag = source[s, d, at] + beside(old[s, d, k], old[s, d, k + 1], old[s, d, k + 2])
                    real, imag = a * real - b * imag, a * imag + b * real
                    to = k if number == 2 else k + 2 * s
                    new[s, c, to] = real
                    new[s, d, to] = imag
                    if number == 2:
                        terms += fwd[s, c, k] * imag + fwd[s, d, k] * real
                if number == 2:
                    grad_ref[:, pl.ds(k + s * (width - 3), 1), :] = (terms * (omega * factor)).reshape(ny, 1, nz)
            return carry
        lax.fori_loop(0, 3, layer, 0, unroll=3)

    sweep(field_0, field_1, 0)
    sweep(field_1, field_2, 1)
    sweep(field_2, field_3, 2)
    stores = [pltpu.make_async_copy(field_3.at[s], adjoint_hbm.at[:, pl.ds(s * (width - 3), 3)], sems.at[6 * s]) for s in range(2)]
    for store in stores:
        store.start()
    core = lax.axis_index("tx") % CORES
    for i in range(ny // CORES):
        keep_ref[i] = grad_ref[CORES * i + core]
        give_ref[i] = grad_ref[CORES * i + 1 - core]
    for store in stores:
        store.wait()


def outer(omega, grad, prev, fwd, halos, from_inner, adjoint, slab_count, factor):
    comps, width, ny, nz = prev.shape
    f32 = jnp.float32
    hbm = pl.BlockSpec(memory_space=pl.ANY)
    vmem = pl.BlockSpec(memory_space=pltpu.VMEM)
    cells = (ny, nz)
    return pl.pallas_call(
        functools.partial(outer_kernel, slab_count, factor),
        out_shape=(jax.ShapeDtypeStruct(prev.shape, f32),) + (jax.ShapeDtypeStruct((ny // CORES, width, nz), f32),) * 2,
        in_specs=[pl.BlockSpec(memory_space=pltpu.SMEM), vmem] + [hbm] * 11,
        out_specs=(hbm, vmem, vmem),
        scratch_shapes=[
            pltpu.VMEM((2, comps, 5) + cells, f32),
            pltpu.VMEM((2, comps, 5) + cells, f32),
            pltpu.VMEM((2, comps, 5) + cells, f32),
            pltpu.VMEM((2, comps, 3) + cells, f32),
            pltpu.VMEM((2, comps, 3) + cells, f32),
            pltpu.VMEM((2, 3) + cells, f32),
            pltpu.VMEM((2, comps, 5) + cells, f32),
            pltpu.VMEM((2, 2, 5) + cells, f32),
            pltpu.VMEM(grad.shape, f32),
            pltpu.SemaphoreType.DMA((12,)),
            pltpu.SemaphoreType.DMA((2, 3)),
        ],
        input_output_aliases={12: 0},
        compiler_params=pltpu.CompilerParams(vmem_limit_bytes=12 * 1024 * 1024),
        cost_estimate=pl.CostEstimate(flops=100_000_000, bytes_accessed=3_000_000, transcendentals=0),
        name="outer",
    )(omega, grad, prev, fwd, *halos, *from_inner, adjoint)


def shards(fwd_field, adj_prev, sigma, omega, res_vals, rec_slab, rec_cell):
    pairs, comps, width, ny, nz = adj_prev.shape
    slabs, groups = lax.axis_size("slab"), lax.axis_size("tx")
    prev, fwd = adj_prev[0], fwd_field[0]
    rows = range(0, slabs, COLUMNS)
    up = [(r + i, r + i + 1) for r in rows for i in range(COLUMNS - 1)]
    down = [(j, i) for i, j in up]
    stage_a = [(r + 3, r) for r in rows] + [(r, r + 3) for r in rows]
    stage_b = [(r + 3, r + 1) for r in rows] + [(r, r + 2) for r in rows]
    cross_a = [(r, r + COLUMNS) for r in rows[:-1]] + [(r + 3, r + 3 - COLUMNS) for r in rows[1:]]
    cross_b = [(r + 1, r + COLUMNS) for r in rows[:-1]] + [(r + 2, r + 3 - COLUMNS) for r in rows[1:]]
    vals = jnp.transpose(res_vals, (1, 0, 2))
    send, part_a, part_b, highest, lowest = pack(vals, rec_slab.reshape(1, -1), rec_cell, prev, sigma, slabs, 4)
    part_a = lax.ppermute(part_a, "slab", stage_a)
    part_b = lax.ppermute(part_b, "slab", stage_b)
    got = lax.all_to_all(send, "slab", split_axis=0, concat_axis=0, tiled=True)
    edge = (lax.axis_index("slab") % COLUMNS) % (COLUMNS - 1) == 0
    part_a = jnp.where(edge, part_a, 0.0)
    part_a, highest, lowest = lax.optimization_barrier((part_a, highest, lowest))
    part_a = lax.ppermute(part_a, "slab", cross_a)
    part_b = lax.ppermute(part_b, "slab", cross_b)
    before = lax.ppermute(highest, "slab", up)
    after = lax.ppermute(lowest, "slab", down)
    factor = 1.0 / (3.0 * pairs * groups) ** 0.5
    adjoint, terms, *from_inner = inner(omega, got, sigma, prev, fwd, factor)
    halos = (before, after, part_a, part_b)
    adjoint, terms, other = outer(omega, terms, prev, fwd, halos, from_inner, adjoint, slabs, factor)
    terms += lax.ppermute(other, "tx", [(i, i ^ 1) for i in range(groups)])
    same_core = [list(range(core, groups, CORES)) for core in range(CORES)]
    parts = lax.all_to_all(terms, "tx", split_axis=0, concat_axis=0, axis_index_groups=same_core, tiled=True)
    gradient = jnp.sum(parts, axis=0)[:, None, :]
    return (adjoint[None], gradient)


def solution(mesh):
    placed = (
        P("tx", None, "slab", None, None),
        P("tx", None, "slab", None, None),
        P("slab", None, None),
        P("tx"),
        P("tx", None, "slab"),
        P("tx", "slab", None),
        P("tx", "slab"),
    )
    return jax.shard_map(
        shards,
        mesh=mesh,
        in_specs=placed,
        out_specs=(P("tx", None, "slab", None, None), P("slab", "tx", None)),
        check_vma=False,
    )
```

```python
import functools

import jax
import jax.numpy as jnp
from jax import lax
from jax.experimental import pallas as pl
from jax.experimental.pallas import tpu as pltpu
from jax.sharding import PartitionSpec as P

SWEEPS = 3
CAP = 32
LANES = 128
CORES = 2
COLUMNS = 4
NT = (((1,), (1,)), ((), ()))


def dot_nt(a, b):
    return lax.dot_general(a, b, NT, preferred_element_type=jnp.float32)


def split_3(value):
    high = value.astype(jnp.bfloat16)
    rest = value - high.astype(jnp.float32)
    middle = rest.astype(jnp.bfloat16)
    low = (rest - middle.astype(jnp.float32)).astype(jnp.bfloat16)
    return high, middle, low


def ones_where(mask):
    return jnp.where(mask, 1.0, 0.0).astype(jnp.bfloat16)


def pack_kernel(
    slabs, vals_ref, slab_ref, cell_ref, prev_hbm, sigma_hbm, fwd_hbm,
    out_ref, part_a_ref, part_b_ref, highest_ref, lowest_ref, rows_ref, sems,
):
    comps, width = prev_hbm.shape[:2]
    copies = []
    for n, (first, ref) in enumerate(((width - SWEEPS, highest_ref), (0, lowest_ref))):
        layers = pl.ds(first, SWEEPS)
        copies.append(pltpu.make_async_copy(prev_hbm.at[:, layers], ref.at[pl.ds(0, comps)], sems.at[2 * n]))
        copies.append(pltpu.make_async_copy(sigma_hbm.at[layers], ref.at[comps], sems.at[2 * n + 1]))
    split = part_a_ref.shape[0]
    last = lax.axis_index("slab") % COLUMNS == COLUMNS - 1

    def parts(first):
        layers = pl.ds(first, SWEEPS)
        return [
            pltpu.make_async_copy(prev_hbm.at[pl.ds(0, split), layers], part_a_ref, sems.at[4]),
            pltpu.make_async_copy(
                prev_hbm.at[pl.ds(split, comps - split), layers], part_b_ref.at[pl.ds(0, comps - split)], sems.at[5]
            ),
            pltpu.make_async_copy(sigma_hbm.at[layers], part_b_ref.at[comps - split], sems.at[6]),
        ]

    @pl.when(last)
    def _():
        for copy in parts(width - SWEEPS):
            copy.start()

    @pl.when(jnp.logical_not(last))
    def _():
        for copy in parts(0):
            copy.start()

    for copy in copies:
        copy.start()

    count = vals_ref.shape[2]
    rows_ref[...] = jnp.zeros_like(rows_ref)
    for c in range(comps):
        rows_ref[c:c + 1, :] = vals_ref[c]
    rows_ref[comps:comps + 1, :] = cell_ref[...].astype(jnp.float32)
    target = slab_ref[...]
    member = ones_where(lax.broadcasted_iota(jnp.int32, (slabs, count), 0) == target)
    earlier = ones_where(
        lax.broadcasted_iota(jnp.int32, (count, count), 0)
        < lax.broadcasted_iota(jnp.int32, (count, count), 1)
    )
    ahead = jnp.dot(member, earlier, preferred_element_type=jnp.float32)
    rank = jnp.sum(ahead * member.astype(jnp.float32), axis=0, keepdims=True)
    key = (target + 1) * CAP + rank.astype(jnp.int32)
    lanes = slabs * CAP + LANES
    chosen = ones_where(lax.broadcasted_iota(jnp.int32, (lanes, count), 0) == key)
    packed = sum(dot_nt(part, chosen) for part in split_3(rows_ref[...]))
    lane = lax.broadcasted_iota(jnp.int32, (8, LANES), 1)
    per_tile = LANES // CAP
    tiles = [packed[:, q * LANES:(q + 1) * LANES] for q in range(lanes // LANES)]
    for d in range(slabs):
        q, m = divmod(d, per_tile)
        if m == 0:
            out_ref[d] = tiles[q]
        else:
            shift = LANES - m * CAP
            out_ref[d] = jnp.where(
                lane < shift, pltpu.roll(tiles[q], shift, 1), pltpu.roll(tiles[q + 1], shift, 1)
            )
    for copy in parts(0) + copies:
        copy.wait()


def pack(vals, target, cells, prev, sigma, fwd, slabs, split):
    comps, _, ny, nz = prev.shape
    f32 = jnp.float32
    hbm = pl.BlockSpec(memory_space=pl.ANY)
    vmem = pl.BlockSpec(memory_space=pltpu.VMEM)
    return pl.pallas_call(
        functools.partial(pack_kernel, slabs),
        out_shape=[jax.ShapeDtypeStruct((slabs, 8, LANES), f32)]
        + [
            jax.ShapeDtypeStruct((blocks, SWEEPS, ny, nz), f32)
            for blocks in (split, comps + 1 - split, comps + 1, comps + 1)
        ],
        in_specs=[vmem, vmem, vmem, hbm, hbm, hbm],
        out_specs=[vmem] * 5,
        scratch_shapes=[pltpu.VMEM((8, vals.shape[2]), f32), pltpu.SemaphoreType.DMA((7,))],
        cost_estimate=pl.CostEstimate(flops=20_000_000, bytes_accessed=100_000, transcendentals=0),
        name="pack",
    )(vals, target, cells, prev, sigma, fwd)


def regroup(got_ref, part):
    lane = lax.broadcasted_iota(jnp.int32, (8, LANES), 1) // CAP
    per_tile = LANES // CAP
    tiles = []
    for first in range(0, got_ref.shape[0], per_tile):
        tile = None
        for j in range(per_tile):
            block = got_ref[first + j]
            shift = (j - part) * CAP % LANES
            if shift:
                block = pltpu.roll(block, shift, 1)
            tile = block if tile is None else jnp.where(lane == j, block, tile)
        tiles.append(tile)
    return jnp.concatenate(tiles, axis=1)


def split_2(value):
    high = value.astype(jnp.bfloat16).astype(jnp.float32)
    return high, value - high


def coefficients(omega, cells):
    beta = omega * cells
    inverse = 1.0 / (36.0 + beta * beta)
    return 6.0 * inverse, beta * inverse


def neighbour_sum(ny, nz):
    ys = lax.broadcasted_iota(jnp.int32, (ny, nz), 0)
    zs = lax.broadcasted_iota(jnp.int32, (ny, nz), 1)
    first_y, last_y, first_z, last_z = ys == 0, ys == ny - 1, zs == 0, zs == nz - 1

    def beside(before, middle, after):
        total = before + after
        total += jnp.where(first_y, 0.0, pltpu.roll(middle, 1, 0)) + jnp.where(last_y, 0.0, pltpu.roll(middle, ny - 1, 0))
        total += jnp.where(first_z, 0.0, pltpu.roll(middle, 1, 1)) + jnp.where(last_z, 0.0, pltpu.roll(middle, nz - 1, 1))
        return total

    return beside


def inner_kernel(
    factor, omega_ref, got_ref, sigma_hbm, prev_hbm, fwd_hbm,
    adjoint_hbm, grad_ref, field_1_hbm, field_2_hbm, source_hbm, coef_hbm,
    field_0, field_1, field_2, field_3, fwd, sig, source, coef, onehot, sems,
):
    comps, width, ny, nz = field_0.shape
    rim = SWEEPS - 1
    load_prev = pltpu.make_async_copy(prev_hbm, field_0, sems.at[0])
    load_fwd = pltpu.make_async_copy(fwd_hbm, fwd, sems.at[1])
    load_sigma = pltpu.make_async_copy(sigma_hbm, sig, sems.at[11])
    for load in (load_prev, load_sigma, load_fwd):
        load.start()

    own = regroup(got_ref, 1)
    count = own.shape[1]
    cell = own[6:7].astype(jnp.int32)
    row, z = cell // nz, cell % nz
    at_z = lax.broadcasted_iota(jnp.int32, (nz, count), 0) == z
    for c in range(comps):
        for half, part in enumerate(split_2(own[c:c + 1])):
            onehot[c * nz:(c + 1) * nz, half * count:(half + 1) * count] = jnp.where(at_z, part, 0.0).astype(jnp.bfloat16)
    block = 4
    for first in range(0, width, block):
        at_row = ones_where(lax.broadcasted_iota(jnp.int32, (block * ny, count), 0) + first * ny == row)
        result = dot_nt(jnp.concatenate([at_row, at_row], axis=1), onehot[...])
        for c in range(comps):
            source[c, rim + first:rim + first + block] = result[:, c * nz:(c + 1) * nz].reshape(block, ny, nz)
    for part, first, at in ((0, width - rim, 0), (2, 0, rim + width)):
        side = regroup(got_ref, part)
        cell = side[6:7].astype(jnp.int32)
        row, z = cell // nz - first * ny, cell % nz
        at_z = ones_where(lax.broadcasted_iota(jnp.int32, (nz, count), 0) == z)
        at_row = lax.broadcasted_iota(jnp.int32, (rim * ny, count), 0) == row
        for c in range(comps):
            high, low = split_2(side[c:c + 1])
            result = dot_nt(jnp.where(at_row, high, 0.0).astype(jnp.bfloat16), at_z)
            result += dot_nt(jnp.where(at_row, low, 0.0).astype(jnp.bfloat16), at_z)
            source[c, at:at + rim] = result.reshape(rim, ny, nz)

    omega = omega_ref[0]
    load_sigma.wait()
    coef[0], coef[1] = coefficients(omega, sig[...])
    beside = neighbour_sum(ny, nz)
    load_prev.wait()

    def sweep(old, new, first, last):
        def layer(i, carry):
            x = i + first
            a, b = coef[0, x], coef[1, x]
            terms = jnp.zeros((ny, nz), jnp.float32)
            for c in range(comps // 2):
                d = c + comps // 2
                real = source[c, x + rim] + beside(old[c, i], old[c, i + 1], old[c, i + 2])
                imag = source[d, x + rim] + beside(old[d, i], old[d, i + 1], old[d, i + 2])
                real, imag = a * real - b * imag, a * imag + b * real
                new[c, i] = real
                new[d, i] = imag
                if last:
                    terms += fwd[c, x] * imag + fwd[d, x] * real
            if last:
                grad_ref[:, pl.ds(x, 1), :] = (terms * (omega * factor)).reshape(ny, 1, nz)
            return carry
        lax.fori_loop(0, new.shape[1], layer, 0, unroll=new.shape[1])

    grad_ref[...] = jnp.zeros_like(grad_ref)
    sweep(field_0, field_1, 1, False)
    sweep(field_1, field_2, 2, False)
    load_fwd.wait()
    sweep(field_2, field_3, 3, True)
    stores = [pltpu.make_async_copy(field_3, adjoint_hbm.at[:, pl.ds(3, width - 6)], sems.at[2])]
    for s in range(2):
        pairs = (
            (field_1.at[:, pl.ds(s * (width - 4), 2)], field_1_hbm.at[s]),
            (field_2.at[:, pl.ds(s * (width - 6), 2)], field_2_hbm.at[s]),
            (source.at[:, pl.ds(s * (width - 1), 5)], source_hbm.at[s]),
            (coef.at[:, pl.ds(s * (width - 3), 3)], coef_hbm.at[s]),
        )
        stores += [pltpu.make_async_copy(src, dst, sems.at[3 + 4 * s + n]) for n, (src, dst) in enumerate(pairs)]
    for store in stores:
        store.start()
    for store in stores:
        store.wait()


def inner(omega, got, sigma, prev, fwd, factor):
    comps, width, ny, nz = prev.shape
    f32 = jnp.float32
    count = got.shape[0] * CAP
    hbm = pl.BlockSpec(memory_space=pl.ANY)
    vmem = pl.BlockSpec(memory_space=pltpu.VMEM)
    cells = (ny, nz)
    return pl.pallas_call(
        functools.partial(inner_kernel, factor),
        out_shape=[jax.ShapeDtypeStruct(shape, f32) for shape in (
            prev.shape, (ny, width, nz), (2, comps, 2) + cells, (2, comps, 2) + cells, (2, comps, 5) + cells, (2, 2, 3) + cells,
        )],
        in_specs=[pl.BlockSpec(memory_space=pltpu.SMEM), vmem, hbm, hbm, hbm],
        out_specs=[hbm, vmem, hbm, hbm, hbm, hbm],
        scratch_shapes=[
            pltpu.VMEM((comps, width) + cells, f32),
            pltpu.VMEM((comps, width - 2) + cells, f32),
            pltpu.VMEM((comps, width - 4) + cells, f32),
            pltpu.VMEM((comps, width - 6) + cells, f32),
            pltpu.VMEM((comps, width) + cells, f32),
            pltpu.VMEM((width,) + cells, f32),
            pltpu.VMEM((comps, width + 4) + cells, f32),
            pltpu.VMEM((2, width) + cells, f32),
            pltpu.VMEM((comps * nz, 2 * count), jnp.bfloat16),
            pltpu.SemaphoreType.DMA((12,)),
        ],
        compiler_params=pltpu.CompilerParams(vmem_limit_bytes=20 * 1024 * 1024),
        cost_estimate=pl.CostEstimate(flops=10_000_000_000, bytes_accessed=30_000_000, transcendentals=0),
        name="inner",
    )(omega, got, sigma, prev, fwd)


def outer_kernel(
    slab_count, factor, omega_ref, inner_grad_ref, prev_hbm, fwd_hbm, before_hbm, after_hbm, direct_hbm, staged_hbm,
    field_1_hbm, field_2_hbm, source_hbm, coef_hbm, inner_adjoint_hbm,
    adjoint_hbm, keep_ref, give_ref,
    field_0, field_1, field_2, field_3, fwd, sig, source, coef, grad_ref, sems, halo_sems,
):
    comps, width, ny, nz = prev_hbm.shape
    me = lax.axis_index("slab")
    column = me % COLUMNS
    loads = []
    for s in range(2):
        pairs = (
            (prev_hbm.at[:, pl.ds(s * (width - 2), 2)], field_0.at[s, :, pl.ds(3 - 3 * s, 2)]),
            (fwd_hbm.at[:, pl.ds(s * (width - 3), 3)], fwd.at[s]),
            (field_1_hbm.at[s], field_1.at[s, :, pl.ds(3 - 3 * s, 2)]),
            (field_2_hbm.at[s], field_2.at[s, :, pl.ds(3 - 3 * s, 2)]),
            (source_hbm.at[s], source.at[s]),
            (coef_hbm.at[s], coef.at[s, :, pl.ds(2 - 2 * s, 3)]),
        )
        loads += [pltpu.make_async_copy(src, dst, sems.at[6 * s + n]) for n, (src, dst) in enumerate(pairs)]
    split = direct_hbm.shape[0]
    for s, (near, far) in enumerate(((before_hbm, 0), (after_hbm, COLUMNS - 1))):
        spot = pl.ds(2 * s, 3)
        at_edge = column == far

        @pl.when(at_edge)
        def _():
            pltpu.make_async_copy(direct_hbm, field_0.at[s, pl.ds(0, split), spot], halo_sems.at[s, 0]).start()
            pltpu.make_async_copy(staged_hbm.at[pl.ds(0, comps - split)], field_0.at[s, pl.ds(split, comps - split), spot], halo_sems.at[s, 1]).start()
            pltpu.make_async_copy(staged_hbm.at[comps - split], sig.at[s], halo_sems.at[s, 2]).start()

        @pl.when(jnp.logical_not(at_edge))
        def _():
            pltpu.make_async_copy(near.at[pl.ds(0, split)], field_0.at[s, pl.ds(0, split), spot], halo_sems.at[s, 0]).start()
            pltpu.make_async_copy(near.at[pl.ds(split, comps - split)], field_0.at[s, pl.ds(split, comps - split), spot], halo_sems.at[s, 1]).start()
            pltpu.make_async_copy(near.at[comps], sig.at[s], halo_sems.at[s, 2]).start()

        loads_of_side = (
            pltpu.make_async_copy(near.at[pl.ds(0, split)], field_0.at[s, pl.ds(0, split), spot], halo_sems.at[s, 0]),
            pltpu.make_async_copy(near.at[pl.ds(split, comps - split)], field_0.at[s, pl.ds(split, comps - split), spot], halo_sems.at[s, 1]),
            pltpu.make_async_copy(near.at[comps], sig.at[s], halo_sems.at[s, 2]),
        )
        if s == 0:
            waits = list(loads_of_side)
        else:
            waits += loads_of_side
    for load in loads:
        load.start()
    grad_ref[...] = inner_grad_ref[...]
    for load in waits + loads:
        load.wait()
    omega = omega_ref[0]
    for s, there in ((0, me > 0), (1, me < slab_count - 1)):
        inside = jnp.where(there, 1.0, 0.0)
        a, b = coefficients(omega, sig[s, 1 - s:3 - s])
        coef[s, 0, 3 * s:3 * s + 2], coef[s, 1, 3 * s:3 * s + 2] = a * inside, b * inside

    beside = neighbour_sum(ny, nz)

    def sweep(old, new, number):
        def layer(k, carry):
            for s in range(2):
                at = k + (number if s == 0 else 2 - number)
                a, b = coef[s, 0, at], coef[s, 1, at]
                terms = jnp.zeros((ny, nz), jnp.float32)
                for c in range(comps // 2):
                    d = c + comps // 2
                    real = source[s, c, at] + beside(old[s, c, k], old[s, c, k + 1], old[s, c, k + 2])
                    imag = source[s, d, at] + beside(old[s, d, k], old[s, d, k + 1], old[s, d, k + 2])
                    real, imag = a * real - b * imag, a * imag + b * real
                    to = k if number == 2 else k + 2 * s
                    new[s, c, to] = real
                    new[s, d, to] = imag
                    if number == 2:
                        terms += fwd[s, c, k] * imag + fwd[s, d, k] * real
                if number == 2:
                    grad_ref[:, pl.ds(k + s * (width - 3), 1), :] = (terms * (omega * factor)).reshape(ny, 1, nz)
            return carry
        lax.fori_loop(0, 3, layer, 0, unroll=3)

    sweep(field_0, field_1, 0)
    sweep(field_1, field_2, 1)
    sweep(field_2, field_3, 2)
    stores = [pltpu.make_async_copy(field_3.at[s], adjoint_hbm.at[:, pl.ds(s * (width - 3), 3)], sems.at[6 * s]) for s in range(2)]
    for store in stores:
        store.start()
    core = lax.axis_index("tx") % CORES
    for i in range(ny // CORES):
        keep_ref[i] = grad_ref[CORES * i + core]
        give_ref[i] = grad_ref[CORES * i + 1 - core]
    for store in stores:
        store.wait()


def outer(omega, grad, prev, fwd, halos, from_inner, adjoint, slab_count, factor):
    comps, width, ny, nz = prev.shape
    f32 = jnp.float32
    hbm = pl.BlockSpec(memory_space=pl.ANY)
    vmem = pl.BlockSpec(memory_space=pltpu.VMEM)
    cells = (ny, nz)
    return pl.pallas_call(
        functools.partial(outer_kernel, slab_count, factor),
        out_shape=(jax.ShapeDtypeStruct(prev.shape, f32),) + (jax.ShapeDtypeStruct((ny // CORES, width, nz), f32),) * 2,
        in_specs=[pl.BlockSpec(memory_space=pltpu.SMEM), vmem] + [hbm] * 11,
        out_specs=(hbm, vmem, vmem),
        scratch_shapes=[
            pltpu.VMEM((2, comps, 5) + cells, f32),
            pltpu.VMEM((2, comps, 5) + cells, f32),
            pltpu.VMEM((2, comps, 5) + cells, f32),
            pltpu.VMEM((2, comps, 3) + cells, f32),
            pltpu.VMEM((2, comps, 3) + cells, f32),
            pltpu.VMEM((2, 3) + cells, f32),
            pltpu.VMEM((2, comps, 5) + cells, f32),
            pltpu.VMEM((2, 2, 5) + cells, f32),
            pltpu.VMEM(grad.shape, f32),
            pltpu.SemaphoreType.DMA((12,)),
            pltpu.SemaphoreType.DMA((2, 3)),
        ],
        input_output_aliases={12: 0},
        compiler_params=pltpu.CompilerParams(vmem_limit_bytes=12 * 1024 * 1024),
        cost_estimate=pl.CostEstimate(flops=100_000_000, bytes_accessed=3_000_000, transcendentals=0),
        name="outer",
    )(omega, grad, prev, fwd, *halos, *from_inner, adjoint)


def shards(fwd_field, adj_prev, sigma, omega, res_vals, rec_slab, rec_cell):
    pairs, comps, width, ny, nz = adj_prev.shape
    slabs, groups = lax.axis_size("slab"), lax.axis_size("tx")
    prev, fwd = adj_prev[0], fwd_field[0]
    rows = range(0, slabs, COLUMNS)
    up = [(r + i, r + i + 1) for r in rows for i in range(COLUMNS - 1)]
    down = [(j, i) for i, j in up]
    stage_a = [(r + 3, r) for r in rows] + [(r, r + 3) for r in rows]
    stage_b = [(r + 3, r + 1) for r in rows] + [(r, r + 2) for r in rows]
    cross_a = [(r, r + COLUMNS) for r in rows[:-1]] + [(r + 3, r + 3 - COLUMNS) for r in rows[1:]]
    cross_b = [(r + 1, r + COLUMNS) for r in rows[:-1]] + [(r + 2, r + 3 - COLUMNS) for r in rows[1:]]
    vals = jnp.transpose(res_vals, (1, 0, 2))
    send, part_a, part_b, highest, lowest = pack(vals, rec_slab.reshape(1, -1), rec_cell, prev, sigma, fwd, slabs, 4)
    part_a = lax.ppermute(part_a, "slab", stage_a)
    part_b = lax.ppermute(part_b, "slab", stage_b)
    got = lax.all_to_all(send, "slab", split_axis=0, concat_axis=0, tiled=True)
    edge = (lax.axis_index("slab") % COLUMNS) % (COLUMNS - 1) == 0
    part_a = jnp.where(edge, part_a, 0.0)
    part_a, highest, lowest = lax.optimization_barrier((part_a, highest, lowest))
    part_a = lax.ppermute(part_a, "slab", cross_a)
    part_b = lax.ppermute(part_b, "slab", cross_b)
    before = lax.ppermute(highest, "slab", up)
    after = lax.ppermute(lowest, "slab", down)
    factor = 1.0 / (3.0 * pairs * groups) ** 0.5
    adjoint, terms, *from_inner = inner(omega, got, sigma, prev, fwd, factor)
    halos = (before, after, part_a, part_b)
    adjoint, terms, other = outer(omega, terms, prev, fwd, halos, from_inner, adjoint, slabs, factor)
    terms += lax.ppermute(other, "tx", [(i, i ^ 1) for i in range(groups)])
    same_core = [list(range(core, groups, CORES)) for core in range(CORES)]
    parts = lax.all_to_all(terms, "tx", split_axis=0, concat_axis=0, axis_index_groups=same_core, tiled=True)
    gradient = jnp.sum(parts, axis=0)[:, None, :]
    return (adjoint[None], gradient)


def solution(mesh):
    placed = (
        P("tx", None, "slab", None, None),
        P("tx", None, "slab", None, None),
        P("slab", None, None),
        P("tx"),
        P("tx", None, "slab"),
        P("tx", "slab", None),
        P("tx", "slab"),
    )
    return jax.shard_map(
        shards,
        mesh=mesh,
        in_specs=placed,
        out_specs=(P("tx", None, "slab", None, None), P("slab", "tx", None)),
        check_vma=False,
    )
```

```python
import functools

import jax
import jax.numpy as jnp
from jax import lax
from jax.experimental import pallas as pl
from jax.experimental.pallas import tpu as pltpu
from jax.sharding import PartitionSpec as P

SWEEPS = 3
CAP = 32
LANES = 128
CORES = 2
COLUMNS = 4
NT = (((1,), (1,)), ((), ()))


def dot_nt(a, b):
    return lax.dot_general(a, b, NT, preferred_element_type=jnp.float32)


def split_3(value):
    high = value.astype(jnp.bfloat16)
    rest = value - high.astype(jnp.float32)
    middle = rest.astype(jnp.bfloat16)
    low = (rest - middle.astype(jnp.float32)).astype(jnp.bfloat16)
    return high, middle, low


def ones_where(mask):
    return jnp.where(mask, 1.0, 0.0).astype(jnp.bfloat16)


def pack_kernel(
    slabs, vals_ref, slab_ref, cell_ref, prev_hbm, sigma_hbm,
    out_ref, part_a_ref, part_b_ref, highest_ref, lowest_ref, rows_ref, sems,
):
    comps, width = prev_hbm.shape[:2]
    copies = []
    for n, (first, ref) in enumerate(((width - SWEEPS, highest_ref), (0, lowest_ref))):
        layers = pl.ds(first, SWEEPS)
        copies.append(pltpu.make_async_copy(prev_hbm.at[:, layers], ref.at[pl.ds(0, comps)], sems.at[2 * n]))
        copies.append(pltpu.make_async_copy(sigma_hbm.at[layers], ref.at[comps], sems.at[2 * n + 1]))
    split = part_a_ref.shape[0]
    last = lax.axis_index("slab") % COLUMNS == COLUMNS - 1

    def parts(first):
        layers = pl.ds(first, SWEEPS)
        return [
            pltpu.make_async_copy(prev_hbm.at[pl.ds(0, split), layers], part_a_ref, sems.at[4]),
            pltpu.make_async_copy(
                prev_hbm.at[pl.ds(split, comps - split), layers], part_b_ref.at[pl.ds(0, comps - split)], sems.at[5]
            ),
            pltpu.make_async_copy(sigma_hbm.at[layers], part_b_ref.at[comps - split], sems.at[6]),
        ]

    @pl.when(last)
    def _():
        for copy in parts(width - SWEEPS):
            copy.start()

    @pl.when(jnp.logical_not(last))
    def _():
        for copy in parts(0):
            copy.start()

    for copy in copies:
        copy.start()

    count = vals_ref.shape[2]
    rows_ref[...] = jnp.zeros_like(rows_ref)
    for c in range(comps):
        rows_ref[c:c + 1, :] = vals_ref[c]
    rows_ref[comps:comps + 1, :] = cell_ref[...].astype(jnp.float32)
    target = slab_ref[...]
    member = ones_where(lax.broadcasted_iota(jnp.int32, (slabs, count), 0) == target)
    earlier = ones_where(
        lax.broadcasted_iota(jnp.int32, (count, count), 0)
        < lax.broadcasted_iota(jnp.int32, (count, count), 1)
    )
    ahead = jnp.dot(member, earlier, preferred_element_type=jnp.float32)
    rank = jnp.sum(ahead * member.astype(jnp.float32), axis=0, keepdims=True)
    key = (target + 1) * CAP + rank.astype(jnp.int32)
    lanes = slabs * CAP + LANES
    chosen = ones_where(lax.broadcasted_iota(jnp.int32, (lanes, count), 0) == key)
    packed = sum(dot_nt(part, chosen) for part in split_3(rows_ref[...]))
    lane = lax.broadcasted_iota(jnp.int32, (8, LANES), 1)
    per_tile = LANES // CAP
    tiles = [packed[:, q * LANES:(q + 1) * LANES] for q in range(lanes // LANES)]
    for d in range(slabs):
        q, m = divmod(d, per_tile)
        if m == 0:
            out_ref[d] = tiles[q]
        else:
            shift = LANES - m * CAP
            out_ref[d] = jnp.where(
                lane < shift, pltpu.roll(tiles[q], shift, 1), pltpu.roll(tiles[q + 1], shift, 1)
            )
    for copy in parts(0) + copies:
        copy.wait()


def pack(vals, target, cells, prev, sigma, slabs, split):
    comps, _, ny, nz = prev.shape
    f32 = jnp.float32
    hbm = pl.BlockSpec(memory_space=pl.ANY)
    vmem = pl.BlockSpec(memory_space=pltpu.VMEM)
    return pl.pallas_call(
        functools.partial(pack_kernel, slabs),
        out_shape=[jax.ShapeDtypeStruct((slabs, 8, LANES), f32)]
        + [
            jax.ShapeDtypeStruct((blocks, SWEEPS, ny, nz), f32)
            for blocks in (split, comps + 1 - split, comps + 1, comps + 1)
        ],
        in_specs=[vmem, vmem, vmem, hbm, hbm],
        out_specs=[vmem] * 5,
        scratch_shapes=[pltpu.VMEM((8, vals.shape[2]), f32), pltpu.SemaphoreType.DMA((7,))],
        cost_estimate=pl.CostEstimate(flops=20_000_000, bytes_accessed=100_000, transcendentals=0),
        name="pack",
    )(vals, target, cells, prev, sigma)


def regroup(got_ref, part):
    lane = lax.broadcasted_iota(jnp.int32, (8, LANES), 1) // CAP
    per_tile = LANES // CAP
    tiles = []
    for first in range(0, got_ref.shape[0], per_tile):
        tile = None
        for j in range(per_tile):
            block = got_ref[first + j]
            shift = (j - part) * CAP % LANES
            if shift:
                block = pltpu.roll(block, shift, 1)
            tile = block if tile is None else jnp.where(lane == j, block, tile)
        tiles.append(tile)
    return jnp.concatenate(tiles, axis=1)


def split_2(value):
    high = value.astype(jnp.bfloat16).astype(jnp.float32)
    return high, value - high


def coefficients(omega, cells):
    beta = omega * cells
    inverse = 1.0 / (36.0 + beta * beta)
    return 6.0 * inverse, beta * inverse


def neighbour_sum(ny, nz):
    ys = lax.broadcasted_iota(jnp.int32, (ny, nz), 0)
    zs = lax.broadcasted_iota(jnp.int32, (ny, nz), 1)
    first_y, last_y, first_z, last_z = ys == 0, ys == ny - 1, zs == 0, zs == nz - 1

    def beside(before, middle, after):
        total = before + after
        total += jnp.where(first_y, 0.0, pltpu.roll(middle, 1, 0)) + jnp.where(last_y, 0.0, pltpu.roll(middle, ny - 1, 0))
        total += jnp.where(first_z, 0.0, pltpu.roll(middle, 1, 1)) + jnp.where(last_z, 0.0, pltpu.roll(middle, nz - 1, 1))
        return total

    return beside


def inner_kernel(
    factor, omega_ref, got_ref, sigma_hbm, prev_hbm, fwd_hbm,
    adjoint_hbm, grad_ref, field_1_hbm, field_2_hbm, source_hbm, coef_hbm,
    field_0, field_1, field_2, field_3, fwd, sig, source, coef, onehot, sems,
):
    comps, width, ny, nz = field_0.shape
    rim = SWEEPS - 1
    load_prev = pltpu.make_async_copy(prev_hbm, field_0, sems.at[0])
    load_fwd = pltpu.make_async_copy(fwd_hbm, fwd, sems.at[1])
    load_sigma = pltpu.make_async_copy(sigma_hbm, sig, sems.at[11])
    for load in (load_prev, load_sigma, load_fwd):
        load.start()

    own = regroup(got_ref, 1)
    count = own.shape[1]
    cell = own[6:7].astype(jnp.int32)
    row, z = cell // nz, cell % nz
    at_z = lax.broadcasted_iota(jnp.int32, (nz, count), 0) == z
    for c in range(comps):
        for half, part in enumerate(split_2(own[c:c + 1])):
            onehot[c * nz:(c + 1) * nz, half * count:(half + 1) * count] = jnp.where(at_z, part, 0.0).astype(jnp.bfloat16)
    block = 4
    for first in range(0, width, block):
        at_row = ones_where(lax.broadcasted_iota(jnp.int32, (block * ny, count), 0) + first * ny == row)
        result = dot_nt(jnp.concatenate([at_row, at_row], axis=1), onehot[...])
        for c in range(comps):
            source[c, rim + first:rim + first + block] = result[:, c * nz:(c + 1) * nz].reshape(block, ny, nz)
    for part, first, at in ((0, width - rim, 0), (2, 0, rim + width)):
        side = regroup(got_ref, part)
        cell = side[6:7].astype(jnp.int32)
        row, z = cell // nz - first * ny, cell % nz
        at_z = ones_where(lax.broadcasted_iota(jnp.int32, (nz, count), 0) == z)
        at_row = lax.broadcasted_iota(jnp.int32, (rim * ny, count), 0) == row
        for c in range(comps):
            high, low = split_2(side[c:c + 1])
            result = dot_nt(jnp.where(at_row, high, 0.0).astype(jnp.bfloat16), at_z)
            result += dot_nt(jnp.where(at_row, low, 0.0).astype(jnp.bfloat16), at_z)
            source[c, at:at + rim] = result.reshape(rim, ny, nz)

    omega = omega_ref[0]
    load_sigma.wait()
    coef[0], coef[1] = coefficients(omega, sig[...])
    beside = neighbour_sum(ny, nz)
    load_prev.wait()

    def sweep(old, new, first, last):
        def layer(i, carry):
            x = i + first
            a, b = coef[0, x], coef[1, x]
            terms = jnp.zeros((ny, nz), jnp.float32)
            for c in range(comps // 2):
                d = c + comps // 2
                real = source[c, x + rim] + beside(old[c, i], old[c, i + 1], old[c, i + 2])
                imag = source[d, x + rim] + beside(old[d, i], old[d, i + 1], old[d, i + 2])
                real, imag = a * real - b * imag, a * imag + b * real
                new[c, i] = real
                new[d, i] = imag
                if last:
                    terms += fwd[c, x] * imag + fwd[d, x] * real
            if last:
                grad_ref[:, pl.ds(x, 1), :] = (terms * (omega * factor)).reshape(ny, 1, nz)
            return carry
        lax.fori_loop(0, new.shape[1], layer, 0, unroll=new.shape[1])

    grad_ref[...] = jnp.zeros_like(grad_ref)
    sweep(field_0, field_1, 1, False)
    sweep(field_1, field_2, 2, False)
    load_fwd.wait()
    sweep(field_2, field_3, 3, True)
    stores = [pltpu.make_async_copy(field_3, adjoint_hbm.at[:, pl.ds(3, width - 6)], sems.at[2])]
    for s in range(2):
        pairs = (
            (field_1.at[:, pl.ds(s * (width - 4), 2)], field_1_hbm.at[s]),
            (field_2.at[:, pl.ds(s * (width - 6), 2)], field_2_hbm.at[s]),
            (source.at[:, pl.ds(s * (width - 1), 5)], source_hbm.at[s]),
            (coef.at[:, pl.ds(s * (width - 3), 3)], coef_hbm.at[s]),
        )
        stores += [pltpu.make_async_copy(src, dst, sems.at[3 + 4 * s + n]) for n, (src, dst) in enumerate(pairs)]
    for store in stores:
        store.start()
    for store in stores:
        store.wait()


def inner(omega, got, sigma, prev, fwd, factor):
    comps, width, ny, nz = prev.shape
    f32 = jnp.float32
    count = got.shape[0] * CAP
    hbm = pl.BlockSpec(memory_space=pl.ANY)
    vmem = pl.BlockSpec(memory_space=pltpu.VMEM)
    cells = (ny, nz)
    return pl.pallas_call(
        functools.partial(inner_kernel, factor),
        out_shape=[jax.ShapeDtypeStruct(shape, f32) for shape in (
            prev.shape, (ny, width, nz), (2, comps, 2) + cells, (2, comps, 2) + cells, (2, comps, 5) + cells, (2, 2, 3) + cells,
        )],
        in_specs=[pl.BlockSpec(memory_space=pltpu.SMEM), vmem, hbm, hbm, hbm],
        out_specs=[hbm, vmem, hbm, hbm, hbm, hbm],
        scratch_shapes=[
            pltpu.VMEM((comps, width) + cells, f32),
            pltpu.VMEM((comps, width - 2) + cells, f32),
            pltpu.VMEM((comps, width - 4) + cells, f32),
            pltpu.VMEM((comps, width - 6) + cells, f32),
            pltpu.VMEM((comps, width) + cells, f32),
            pltpu.VMEM((width,) + cells, f32),
            pltpu.VMEM((comps, width + 4) + cells, f32),
            pltpu.VMEM((2, width) + cells, f32),
            pltpu.VMEM((comps * nz, 2 * count), jnp.bfloat16),
            pltpu.SemaphoreType.DMA((12,)),
        ],
        compiler_params=pltpu.CompilerParams(vmem_limit_bytes=20 * 1024 * 1024),
        cost_estimate=pl.CostEstimate(flops=10_000_000_000, bytes_accessed=8_000_000, transcendentals=0),
        name="inner",
    )(omega, got, sigma, prev, fwd)


def outer_kernel(
    slab_count, factor, omega_ref, inner_grad_ref, prev_hbm, fwd_hbm, before_hbm, after_hbm, direct_hbm, staged_hbm,
    field_1_hbm, field_2_hbm, source_hbm, coef_hbm, inner_adjoint_hbm,
    adjoint_hbm, keep_ref, give_ref,
    field_0, field_1, field_2, field_3, fwd, sig, source, coef, grad_ref, sems, halo_sems,
):
    comps, width, ny, nz = prev_hbm.shape
    me = lax.axis_index("slab")
    column = me % COLUMNS
    loads = []
    for s in range(2):
        pairs = (
            (prev_hbm.at[:, pl.ds(s * (width - 2), 2)], field_0.at[s, :, pl.ds(3 - 3 * s, 2)]),
            (fwd_hbm.at[:, pl.ds(s * (width - 3), 3)], fwd.at[s]),
            (field_1_hbm.at[s], field_1.at[s, :, pl.ds(3 - 3 * s, 2)]),
            (field_2_hbm.at[s], field_2.at[s, :, pl.ds(3 - 3 * s, 2)]),
            (source_hbm.at[s], source.at[s]),
            (coef_hbm.at[s], coef.at[s, :, pl.ds(2 - 2 * s, 3)]),
        )
        loads += [pltpu.make_async_copy(src, dst, sems.at[6 * s + n]) for n, (src, dst) in enumerate(pairs)]
    split = direct_hbm.shape[0]
    for s, (near, far) in enumerate(((before_hbm, 0), (after_hbm, COLUMNS - 1))):
        spot = pl.ds(2 * s, 3)
        at_edge = column == far

        @pl.when(at_edge)
        def _():
            pltpu.make_async_copy(direct_hbm, field_0.at[s, pl.ds(0, split), spot], halo_sems.at[s, 0]).start()
            pltpu.make_async_copy(staged_hbm.at[pl.ds(0, comps - split)], field_0.at[s, pl.ds(split, comps - split), spot], halo_sems.at[s, 1]).start()
            pltpu.make_async_copy(staged_hbm.at[comps - split], sig.at[s], halo_sems.at[s, 2]).start()

        @pl.when(jnp.logical_not(at_edge))
        def _():
            pltpu.make_async_copy(near.at[pl.ds(0, split)], field_0.at[s, pl.ds(0, split), spot], halo_sems.at[s, 0]).start()
            pltpu.make_async_copy(near.at[pl.ds(split, comps - split)], field_0.at[s, pl.ds(split, comps - split), spot], halo_sems.at[s, 1]).start()
            pltpu.make_async_copy(near.at[comps], sig.at[s], halo_sems.at[s, 2]).start()

        loads_of_side = (
            pltpu.make_async_copy(near.at[pl.ds(0, split)], field_0.at[s, pl.ds(0, split), spot], halo_sems.at[s, 0]),
            pltpu.make_async_copy(near.at[pl.ds(split, comps - split)], field_0.at[s, pl.ds(split, comps - split), spot], halo_sems.at[s, 1]),
            pltpu.make_async_copy(near.at[comps], sig.at[s], halo_sems.at[s, 2]),
        )
        if s == 0:
            waits = list(loads_of_side)
        else:
            waits += loads_of_side
    for load in loads:
        load.start()
    grad_ref[...] = inner_grad_ref[...]
    for load in waits + loads:
        load.wait()
    omega = omega_ref[0]
    for s, there in ((0, me > 0), (1, me < slab_count - 1)):
        inside = jnp.where(there, 1.0, 0.0)
        a, b = coefficients(omega, sig[s, 1 - s:3 - s])
        coef[s, 0, 3 * s:3 * s + 2], coef[s, 1, 3 * s:3 * s + 2] = a * inside, b * inside

    beside = neighbour_sum(ny, nz)

    def sweep(old, new, number):
        def layer(k, carry):
            for s in range(2):
                at = k + (number if s == 0 else 2 - number)
                a, b = coef[s, 0, at], coef[s, 1, at]
                terms = jnp.zeros((ny, nz), jnp.float32)
                for c in range(comps // 2):
                    d = c + comps // 2
                    real = source[s, c, at] + beside(old[s, c, k], old[s, c, k + 1], old[s, c, k + 2])
                    imag = source[s, d, at] + beside(old[s, d, k], old[s, d, k + 1], old[s, d, k + 2])
                    real, imag = a * real - b * imag, a * imag + b * real
                    to = k if number == 2 else k + 2 * s
                    new[s, c, to] = real
                    new[s, d, to] = imag
                    if number == 2:
                        terms += fwd[s, c, k] * imag + fwd[s, d, k] * real
                if number == 2:
                    grad_ref[:, pl.ds(k + s * (width - 3), 1), :] = (terms * (omega * factor)).reshape(ny, 1, nz)
            return carry
        lax.fori_loop(0, 3, layer, 0, unroll=3)

    sweep(field_0, field_1, 0)
    sweep(field_1, field_2, 1)
    sweep(field_2, field_3, 2)
    stores = [pltpu.make_async_copy(field_3.at[s], adjoint_hbm.at[:, pl.ds(s * (width - 3), 3)], sems.at[6 * s]) for s in range(2)]
    for store in stores:
        store.start()
    core = lax.axis_index("tx") % CORES
    for i in range(ny // CORES):
        keep_ref[i] = grad_ref[CORES * i + core]
        give_ref[i] = grad_ref[CORES * i + 1 - core]
    for store in stores:
        store.wait()


def outer(omega, grad, prev, fwd, halos, from_inner, adjoint, slab_count, factor):
    comps, width, ny, nz = prev.shape
    f32 = jnp.float32
    hbm = pl.BlockSpec(memory_space=pl.ANY)
    vmem = pl.BlockSpec(memory_space=pltpu.VMEM)
    cells = (ny, nz)
    return pl.pallas_call(
        functools.partial(outer_kernel, slab_count, factor),
        out_shape=(jax.ShapeDtypeStruct(prev.shape, f32),) + (jax.ShapeDtypeStruct((ny // CORES, width, nz), f32),) * 2,
        in_specs=[pl.BlockSpec(memory_space=pltpu.SMEM), vmem] + [hbm] * 11,
        out_specs=(hbm, vmem, vmem),
        scratch_shapes=[
            pltpu.VMEM((2, comps, 5) + cells, f32),
            pltpu.VMEM((2, comps, 5) + cells, f32),
            pltpu.VMEM((2, comps, 5) + cells, f32),
            pltpu.VMEM((2, comps, 3) + cells, f32),
            pltpu.VMEM((2, comps, 3) + cells, f32),
            pltpu.VMEM((2, 3) + cells, f32),
            pltpu.VMEM((2, comps, 5) + cells, f32),
            pltpu.VMEM((2, 2, 5) + cells, f32),
            pltpu.VMEM(grad.shape, f32),
            pltpu.SemaphoreType.DMA((12,)),
            pltpu.SemaphoreType.DMA((2, 3)),
        ],
        input_output_aliases={12: 0},
        compiler_params=pltpu.CompilerParams(vmem_limit_bytes=12 * 1024 * 1024),
        cost_estimate=pl.CostEstimate(flops=3_000_000_000, bytes_accessed=300_000, transcendentals=0),
        name="outer",
    )(omega, grad, prev, fwd, *halos, *from_inner, adjoint)


def shards(fwd_field, adj_prev, sigma, omega, res_vals, rec_slab, rec_cell):
    pairs, comps, width, ny, nz = adj_prev.shape
    slabs, groups = lax.axis_size("slab"), lax.axis_size("tx")
    prev, fwd = adj_prev[0], fwd_field[0]
    rows = range(0, slabs, COLUMNS)
    up = [(r + i, r + i + 1) for r in rows for i in range(COLUMNS - 1)]
    down = [(j, i) for i, j in up]
    stage_a = [(r + 3, r) for r in rows] + [(r, r + 3) for r in rows]
    stage_b = [(r + 3, r + 1) for r in rows] + [(r, r + 2) for r in rows]
    cross_a = [(r, r + COLUMNS) for r in rows[:-1]] + [(r + 3, r + 3 - COLUMNS) for r in rows[1:]]
    cross_b = [(r + 1, r + COLUMNS) for r in rows[:-1]] + [(r + 2, r + 3 - COLUMNS) for r in rows[1:]]
    vals = jnp.transpose(res_vals, (1, 0, 2))
    send, part_a, part_b, highest, lowest = pack(vals, rec_slab.reshape(1, -1), rec_cell, prev, sigma, slabs, 4)
    part_a = lax.ppermute(part_a, "slab", stage_a)
    part_b = lax.ppermute(part_b, "slab", stage_b)
    got = lax.all_to_all(send, "slab", split_axis=0, concat_axis=0, tiled=True)
    edge = (lax.axis_index("slab") % COLUMNS) % (COLUMNS - 1) == 0
    part_a = jnp.where(edge, part_a, 0.0)
    part_a, highest, lowest = lax.optimization_barrier((part_a, highest, lowest))
    part_a = lax.ppermute(part_a, "slab", cross_a)
    part_b = lax.ppermute(part_b, "slab", cross_b)
    before = lax.ppermute(highest, "slab", up)
    after = lax.ppermute(lowest, "slab", down)
    factor = 1.0 / (3.0 * pairs * groups) ** 0.5
    adjoint, terms, *from_inner = inner(omega, got, sigma, prev, fwd, factor)
    halos = (before, after, part_a, part_b)
    adjoint, terms, other = outer(omega, terms, prev, fwd, halos, from_inner, adjoint, slabs, factor)
    terms += lax.ppermute(other, "tx", [(i, i ^ 1) for i in range(groups)])
    same_core = [list(range(core, groups, CORES)) for core in range(CORES)]
    parts = lax.all_to_all(terms, "tx", split_axis=0, concat_axis=0, axis_index_groups=same_core, tiled=True)
    gradient = jnp.sum(parts, axis=0)[:, None, :]
    return (adjoint[None], gradient)


def solution(mesh):
    placed = (
        P("tx", None, "slab", None, None),
        P("tx", None, "slab", None, None),
        P("slab", None, None),
        P("tx"),
        P("tx", None, "slab"),
        P("tx", "slab", None),
        P("tx", "slab"),
    )
    return jax.shard_map(
        shards,
        mesh=mesh,
        in_specs=placed,
        out_specs=(P("tx", None, "slab", None, None), P("slab", "tx", None)),
        check_vma=False,
    )
```
